32 devices in a mesh: pool: 2 (over y), train: 16 (over z, x, core), cand: 1.
Axes of the slice: x: 2, y: 2, z: 4, core: 2. Of those that a mesh axis runs over, the one named last changes fastest.
Arguments:
- cand_desc: bfloat16 [4096, 768], P(('pool', 'cand', 'train')), parts along dimension 0, as said below
- struct_id: int32 [4096], P(('pool', 'cand', 'train')), parts along dimension 0, may hold values from 0 to 127, as said below
- train_desc: bfloat16 [24576, 768], P(('pool', 'train')), parts along dimension 0, as said below
- lanczos: bfloat16 [24576, 128], P(('pool', 'train')), parts along dimension 0, may hold values from -0.011962891 to 0.011962891
- mean_weight: bfloat16 [24576], P(('pool', 'train')), parts along dimension 0, may hold values from -0.29882812 to 0.29882812
Outputs:
- pred_mean: float32 [256], P(('pool', 'cand', 'train')), parts along dimension 0
- covariance: float32 [2, 128, 128], P(('pool', 'cand'), 'train'), parts along dimension 0
The draws below stay inside these ranges and needn't reach their ends.
There are 2 independent parts, one for each index of `pool`. The reference program is written for one: setup_inputs(seed, part) draws one part's arguments, and reference() takes and returns one part's arrays. A program takes and returns all parts, laid end to end along the dimension named above; each array names one. Nothing has to cross between parts.
Inputs may be any that keep to these rules, and one draw needn't show every extreme that they name: `struct_id`: rows come in aligned blocks of 128; block b holds structures b * 8 to b * 8 + 7 in increasing order, each with at least one row. `cand_desc`: all entries are positive. `train_desc`: all entries are positive.
All inputs are finite; a program needn't handle non-finite values.
Results may differ from the reference program's by a relative error of at most 0.0015.
The reference program's roundings to bfloat16 on the way (of `cand_unit`, `train_unit` and `kernel_rows`) count: a program that leaves them out, or rounds other values in their place, can miss the bound.
Values may be sent and summed in bfloat16 or wider, within the bound.
No kernel may reach another device: no remote copies, remote signals or barrier semaphores. Data moves between devices by JAX's collectives and lax.ppermute only.
A program may use at most 64 MiB of HBM per device.

```python
import math
import jax
import jax.numpy as jnp
from jax import lax

D = 768
RANK = 128
BLK = 128
SPB = 8
CE_DEV = 128
TRAIN = 12288
CENV = 2048
STRUCTS = 128
SB = 128
N_TRAIN = 16
N_CAND = 1


def column_scale(key):
    column_key = jax.random.fold_in(key, 11)
    return jnp.exp(jax.random.uniform(column_key, (D,), jnp.float32, 0.0, math.log(10.0)))


def draw_cand_desc(key, part):
    columns = column_scale(key)
    key = jax.random.fold_in(key, 1)
    key_rows, key_entries = jax.random.split(key)
    row_scale = jnp.exp(jax.random.uniform(key_rows, (CENV, 1), jnp.float32, 0.0, math.log(10.0)))
    entries = jnp.exp(jax.random.uniform(key_entries, (CENV, D), jnp.float32, math.log(0.05), 0.0))
    return (entries * columns[None, :] * row_scale).astype(jnp.bfloat16)


def draw_train_desc(key, part):
    columns = column_scale(key)
    key = jax.random.fold_in(key, 2)
    key_rows, key_entries = jax.random.split(key)
    row_scale = jnp.exp(jax.random.uniform(key_rows, (TRAIN, 1), jnp.float32, 0.0, math.log(10.0)))
    entries = jnp.exp(jax.random.uniform(key_entries, (TRAIN, D), jnp.float32, math.log(0.05), 0.0))
    return (entries * columns[None, :] * row_scale).astype(jnp.bfloat16)


def draw_struct_id(key, part):
    key = jax.random.fold_in(key, 3)
    block_count = CENV // BLK
    block_keys = jax.random.split(key, block_count)
    cut_points = jax.vmap(lambda subkey: jax.random.permutation(subkey, BLK - 1)[:SPB - 1] + 1)(block_keys)
    position = jnp.arange(BLK, dtype=jnp.int32)
    within = jnp.sum((cut_points[:, None, :] <= position[None, :, None]).astype(jnp.int32), axis=2)
    struct_ids = jnp.arange(block_count, dtype=jnp.int32)[:, None] * SPB + within
    return struct_ids.reshape(CENV).astype(jnp.int32)


def levels(own_key, extent, cuts, low, top_value):
    def one(dim, parts):
        steps = jax.random.uniform(jax.random.fold_in(jax.random.fold_in(own_key, 6), dim), (parts,), jnp.float32, low / len(cuts), top_value / len(cuts))
        return jnp.repeat(jnp.exp(steps), extent[dim] // parts).reshape((-1,) + (1,) * (len(extent) - dim - 1))

    level = one(*cuts[0])
    for cut in cuts[1:]:
        level = level * one(*cut)
    return level


def scatter_about(key, shape, deviation, most, cuts=(), kind=jnp.bfloat16):
    result = jax.random.normal(key, shape, jnp.float32) * deviation
    if len(cuts) > 0:
        result = levels(key, shape, cuts, -0.22, 0.18) * result
    return jnp.clip(result, min=-most, max=most).astype(kind)


def setup_inputs(seed: int = 0, part: int = 0) -> dict:
    keys = jax.random.split(jax.random.key(seed), 6)
    part_keys = jax.random.split(jax.random.fold_in(keys[5], part), 6)
    return {
        "cand_desc": draw_cand_desc(jax.random.fold_in(jax.random.fold_in(keys[5], part), 71), part),
        "struct_id": draw_struct_id(jax.random.fold_in(jax.random.fold_in(keys[5], part), 71), part),
        "train_desc": draw_train_desc(jax.random.fold_in(jax.random.fold_in(keys[5], part), 71), part),
        "lanczos": scatter_about(part_keys[3], (TRAIN, RANK), 0.002, 0.011962891, ((0, 16),)),
        "mean_weight": scatter_about(part_keys[4], (TRAIN,), 0.05, 0.29882812, ((0, 16),)),
    }


EPSILON = 1e-06

def unit_rows(values):
    wide = values.astype(jnp.float32)
    scale = lax.rsqrt(lax.optimization_barrier(jnp.mean(wide * wide, axis=1, keepdims=True)) + EPSILON)
    return (wide * scale).astype(jnp.bfloat16)

def kernel_block(left, right):
    products = lax.dot_general(left, right, (((1,), (1,)), ((), ())), preferred_element_type=jnp.float32)
    cosine = products / left.shape[1]
    square = cosine * cosine
    return square * square

def structure_weight(struct_ids, count):
    within = struct_ids - struct_ids[0]
    member = (jnp.arange(count, dtype=jnp.int32)[:, None] == within[None, :]).astype(jnp.float32)
    return member / lax.optimization_barrier(jnp.sum(member, axis=1, keepdims=True))

def reference(cand_desc, struct_id, train_desc, lanczos, mean_weight):
    cand_unit = unit_rows(cand_desc)
    train_unit = unit_rows(train_desc)
    batch_rows = CE_DEV * N_TRAIN
    rows = cand_unit.reshape(N_CAND, batch_rows, D)
    owners = struct_id.reshape(N_CAND, batch_rows)

    def one_batch(item):
        members, struct_ids = item
        kernel_rows = kernel_block(members, train_unit).astype(jnp.bfloat16)
        projection = jnp.dot(kernel_rows, lanczos, preferred_element_type=jnp.float32)
        mean_terms = jnp.dot(kernel_rows, mean_weight, preferred_element_type=jnp.float32)
        weight = structure_weight(struct_ids, SB)
        high = lax.Precision.HIGHEST
        struct_q = jnp.dot(weight, projection, precision=high)
        struct_mean = jnp.dot(weight, mean_terms, precision=high)
        pairs = kernel_block(members, members)
        prior = jnp.dot(jnp.dot(weight, pairs, precision=high), weight.T, precision=high)
        covariance = prior - jnp.dot(struct_q, struct_q.T, precision=high)
        return (struct_mean, covariance)
    means, covariance = lax.map(one_batch, (rows, owners))
    return (means.reshape(STRUCTS), covariance)
```

```python
import functools

import jax
import jax.numpy as jnp
from jax import lax
from jax.experimental import pallas as pl
from jax.experimental.pallas import tpu as pltpu
from jax.sharding import PartitionSpec as P

SPB = 8
EPSILON = 1e-06
HIGH = lax.Precision.HIGHEST
LANES = 128
VMEM = pl.BlockSpec(memory_space=pltpu.VMEM)


def unit_rows(values):
    wide = values.astype(jnp.float32)
    scale = lax.rsqrt(jnp.mean(wide * wide, axis=1, keepdims=True) + EPSILON)
    return (wide * scale).astype(jnp.bfloat16)


def contract_lanes(left, right, precision=None):
    return lax.dot_general(
        left,
        right,
        (((1,), (1,)), ((), ())),
        preferred_element_type=jnp.float32,
        precision=precision,
    )


def pack_cand(cand_ref, ids_ref, out_ref):
    rows, width = cand_ref.shape
    unit = unit_rows(cand_ref[...])
    for chunk in range(width // LANES):
        out_ref[chunk * rows : (chunk + 1) * rows, :] = unit[
            :, chunk * LANES : (chunk + 1) * LANES
        ]
    within = (ids_ref[...] - ids_ref[0, 0]).astype(jnp.float32)
    out_ref[width // LANES * rows :, :] = jnp.broadcast_to(within, (16, rows)).astype(
        jnp.bfloat16
    )


def pack_train(train_ref, lanczos_ref, weight_ref, out_ref):
    rows, width = train_ref.shape
    rank = lanczos_ref.shape[1]
    step = 128

    def one(start):
        part = pl.ds(pl.multiple_of(start * step, step), step)
        out_ref[part, :] = unit_rows(train_ref[part, :])

    pl.loop(0, rows // step)(one)
    out_ref[rows : rows + rank, :] = (
        lanczos_ref[...].astype(jnp.float32).T.astype(jnp.bfloat16)
    )
    out_ref[rows + rank :, :] = jnp.broadcast_to(
        weight_ref[...].astype(jnp.float32), (16, width)
    ).astype(jnp.bfloat16)


def unpack(ref, rows, chunks):
    return jnp.concatenate(
        [ref[c * rows : (c + 1) * rows, :] for c in range(chunks)], axis=1
    )


def quartic(products, width):
    cosine = products * (1.0 / width)
    square = cosine * cosine
    return square * square


def member_of(ids, base, count):
    row = lax.broadcasted_iota(jnp.int32, (count, ids.shape[1]), 0)
    return (row == ids.astype(jnp.int32) + base).astype(jnp.float32)


def group_kernel(
    masks, chips, rows, width, rank, first, own_ref, sib_ref, one_ref, two_ref,
    town_ref, tsib_ref, *rest
):
    if first:
        q_out, prior_out = rest
    else:
        q_in, prior_in, q_out, prior_out = rest
    chunks = width // LANES
    me = lax.axis_index("train")
    chip, core = me // 2, me % 2
    blocks = jnp.concatenate(
        [unpack(one_ref, rows, chunks), unpack(two_ref, rows, chunks)], axis=0
    )
    id_rows = [
        ref[chunks * rows : chunks * rows + 1, :].astype(jnp.float32)
        for ref in (one_ref, two_ref)
    ]
    owners = [lax.bitwise_xor(chip, mask) for mask in masks]
    structs = chips * SPB
    member = jnp.concatenate(
        [member_of(i, o * SPB, structs) for i, o in zip(id_rows, owners)], axis=1
    )
    scale = 1.0 / jnp.maximum(jnp.sum(member, axis=1, keepdims=True), 1.0)
    proj = None
    for ref in (town_ref, tsib_ref):
        train_rows = ref.shape[0] - rank - 16
        kernel_rows = quartic(
            contract_lanes(ref[:train_rows, :], blocks), width
        ).astype(jnp.bfloat16)
        term = jnp.dot(
            ref[train_rows:, :], kernel_rows, preferred_element_type=jnp.float32
        )
        proj = term if proj is None else proj + term
    q = contract_lanes(member, proj[:rank], HIGH) * scale
    means = contract_lanes(proj[rank : rank + 8], member * scale, HIGH)
    if structs < LANES:
        means = jnp.concatenate(
            [means, jnp.zeros((8, LANES - structs), jnp.float32)], axis=1
        )
    q_all = jnp.concatenate([q, means], axis=0)

    chip_rows = jnp.concatenate(
        [unpack(own_ref, rows, chunks), unpack(sib_ref, rows, chunks)], axis=0
    )
    pairs = quartic(contract_lanes(chip_rows, blocks), width)
    none = jnp.zeros((SPB, rows), jnp.float32)
    own_id, sib_id = [
        ref[chunks * rows : chunks * rows + 1, :].astype(jnp.float32)
        for ref in (own_ref, sib_ref)
    ]
    left = jnp.concatenate(
        [
            jnp.concatenate([member_of(own_id, 0, SPB), none], axis=1),
            jnp.concatenate([none, member_of(sib_id, 0, SPB)], axis=1),
        ],
        axis=0,
    )
    left = left / jnp.sum(left, axis=1, keepdims=True)
    wide = jnp.concatenate(
        [
            member_of(i, (o * 2 + core) * SPB, 2 * structs)
            for i, o in zip(id_rows, owners)
        ],
        axis=1,
    )
    wide = wide / jnp.maximum(jnp.sum(wide, axis=1, keepdims=True), 1.0)
    half = jnp.dot(left, pairs, preferred_element_type=jnp.float32, precision=HIGH)
    prior = contract_lanes(half, wide, HIGH)
    if first:
        q_out[...] = q_all
        prior_out[...] = prior
    else:
        q_out[...] = q_in[...] + q_all
        prior_out[...] = prior_in[...] + prior


def finish(q_ref, other_ref, mine_ref, theirs_ref, mean_ref, cov_ref, all_ref):
    structs = q_ref.shape[0] - 8
    me = lax.axis_index("train")
    chip, core = me // 2, me % 2
    for p in range(structs // SPB):
        rows = slice(p * SPB, (p + 1) * SPB)
        here = pl.multiple_of((2 * p + core) * SPB, SPB)
        there = pl.multiple_of((2 * p + 1 - core) * SPB, SPB)
        all_ref[pl.ds(here, SPB), :] = q_ref[rows, :]
        all_ref[pl.ds(there, SPB), :] = other_ref[rows, :]
    own = q_ref[pl.ds(pl.multiple_of(chip * SPB, SPB), SPB), :]
    cov_ref[...] = mine_ref[...] + theirs_ref[...] - contract_lanes(own, all_ref[...], HIGH)
    lane = lax.broadcasted_iota(jnp.int32, (SPB, LANES), 1)
    row = lax.broadcasted_iota(jnp.int32, (SPB, LANES), 0)
    means = jnp.broadcast_to(q_ref[structs : structs + 1, :], (SPB, LANES))
    column = jnp.sum(jnp.where(lane == chip * SPB + row, means, 0.0), axis=1, keepdims=True)
    mean_ref[...] = jnp.sum(jnp.where(lane == row, column, 0.0), axis=0, keepdims=True)


def call(kernel, shapes, count, flops=0, transfers=0, scratch=()):
    many = isinstance(shapes, (tuple, list))
    return pl.pallas_call(
        kernel,
        out_shape=shapes,
        in_specs=[VMEM] * count,
        out_specs=[VMEM] * len(shapes) if many else VMEM,
        scratch_shapes=scratch,
        cost_estimate=pl.CostEstimate(
            flops=flops, bytes_accessed=transfers, transcendentals=0
        ),
        compiler_params=pltpu.CompilerParams(vmem_limit_bytes=24 * 2**20),
    )


def body(size, cand_desc, struct_id, train_desc, lanczos, mean_weight):
    rows, width = cand_desc.shape
    train_rows, rank = lanczos.shape
    chips = size // 2
    structs = chips * SPB

    def swap(value, mask):
        return lax.ppermute(value, "train", [(i, i ^ mask) for i in range(size)])

    own = call(
        pack_cand,
        jax.ShapeDtypeStruct((rows * width // LANES + 16, LANES), jnp.bfloat16),
        2,
    )(cand_desc, struct_id.reshape(1, rows))
    blocks = {0: own}
    if size == 16:
        for mask in (6, 4, 2, 1):
            blocks[mask] = swap(own, 2 * mask)
        for mask in (2, 4, 6):
            blocks[mask + 1] = swap(blocks[mask], 2)
        groups = [(0, 1), (2, 3), (4, 5), (6, 7)]
    else:
        for mask in range(1, chips):
            blocks[mask] = swap(own, 2 * mask)
        groups = [(m, m + 1) for m in range(0, chips, 2)]
    sib = swap(own, 1)
    train_own = call(
        pack_train,
        jax.ShapeDtypeStruct((train_rows + rank + 16, width), jnp.bfloat16),
        3,
    )(train_desc, lanczos, mean_weight.reshape(1, train_rows))
    train_sib = swap(train_own, 1)

    q_shape = jax.ShapeDtypeStruct((structs + 8, LANES), jnp.float32)
    prior_shape = jax.ShapeDtypeStruct((2 * SPB, 2 * structs), jnp.float32)
    state = ()
    for masks in groups:
        kernel = functools.partial(
            group_kernel, masks, chips, rows, width, rank, not state
        )
        state = call(
            kernel,
            (q_shape, prior_shape),
            6 + len(state),
            flops=2 * 2 * rows * 2 * train_rows * (width + 2 * rank),
        )(own, sib, blocks[masks[0]], blocks[masks[1]], train_own, train_sib, *state)
    q, prior = state
    theirs = swap(prior[SPB:], 1)
    mask = 2
    while mask < size:
        q = q + swap(q, mask)
        mask *= 2
    other = swap(q, 1)
    mean, covariance = call(
        finish,
        (
            jax.ShapeDtypeStruct((1, LANES), jnp.float32),
            jax.ShapeDtypeStruct((SPB, 2 * structs), jnp.float32),
        ),
        4,
        scratch=[pltpu.VMEM((2 * structs, LANES), jnp.float32)],
    )(q, other, prior[:SPB], theirs)
    return mean[0, :SPB], covariance[None]


def solution(mesh):
    placed = (
        P(("pool", "cand", "train"), None),
        P(("pool", "cand", "train")),
        P(("pool", "train"), None),
        P(("pool", "train"), None),
        P(("pool", "train")),
    )
    return jax.shard_map(
        functools.partial(body, mesh.shape["train"]),
        mesh=mesh,
        in_specs=placed,
        out_specs=(P(("pool", "cand", "train")), P(("pool", "cand"), "train", None)),
        check_vma=False,
    )
```

```python
import functools

import jax
import jax.numpy as jnp
from jax import lax
from jax.experimental import pallas as pl
from jax.experimental.pallas import tpu as pltpu
from jax.sharding import PartitionSpec as P

SPB = 8
EPSILON = 1e-06
LANES = 128
TAIL = 16
VMEM = pl.BlockSpec(memory_space=pltpu.VMEM)
HBM = pl.BlockSpec(memory_space=pltpu.HBM)


def unit_rows(values):
    wide = values.astype(jnp.float32)
    scale = lax.rsqrt(jnp.mean(wide * wide, axis=1, keepdims=True) + EPSILON)
    return (wide * scale).astype(jnp.bfloat16)


def product(left, right, dims=((1,), (0,))):
    return lax.dot_general(
        left, right, (dims, ((), ())), preferred_element_type=jnp.float32
    )


def thirds(value):
    parts = []
    for _ in range(3):
        part = value.astype(jnp.bfloat16)
        parts.append(part)
        value = value - part.astype(jnp.float32)
    return parts


def pack_cand(cand_ref, ids_ref, out_ref, raw, ids, sems):
    rows, width = raw.shape
    copies = [
        pltpu.make_async_copy(cand_ref, raw, sems.at[0]),
        pltpu.make_async_copy(ids_ref, ids, sems.at[1]),
    ]
    for copy in copies:
        copy.start()
    for copy in copies:
        copy.wait()
    out_ref[:width, :] = unit_rows(raw[...]).T
    within = (ids[...] - ids[0, 0]).astype(jnp.float32)
    out_ref[width:, :] = jnp.broadcast_to(within, (TAIL, rows)).astype(jnp.bfloat16)


def pack_train(*refs):
    for train_ref, lanczos_ref, weight_ref, out_ref in (
        refs[:3] + refs[6:7],
        refs[3:6] + refs[7:],
    ):
        count, rank = lanczos_ref.shape
        step = count // 6
        for i in range(6):
            part = slice(i * step, (i + 1) * step)
            out_ref[part, :] = unit_rows(train_ref[part, :])
        out_ref[count : count + rank, :] = lanczos_ref[...].T
        out_ref[count + rank :, :] = jnp.broadcast_to(
            weight_ref[...].astype(jnp.float32).reshape(1, count), (TAIL, count)
        ).astype(jnp.bfloat16)


def copy_after(value_ref, _, out_ref):
    out_ref[...] = value_ref[...]


def quartic(products, width):
    cosine = products * (1.0 / width)
    square = cosine * cosine
    return square * square


def member_of(ref, base, count):
    ids = ref[ref.shape[0] - TAIL :, :][:1].astype(jnp.int32) + base
    row = lax.broadcasted_iota(jnp.int32, (count, ids.shape[1]), 0)
    return (row == ids).astype(jnp.bfloat16)


def project(masks, chips, width, rank, first, one_ref, two_ref, town_ref, tsib_ref, *rest):
    chip = lax.axis_index("train") // 2
    pair = jnp.concatenate([one_ref[:width, :], two_ref[:width, :]], axis=1)
    structs = chips * SPB
    member = jnp.concatenate(
        [
            member_of(ref, lax.bitwise_xor(chip, mask) * SPB, structs)
            for ref, mask in zip((one_ref, two_ref), masks)
        ],
        axis=1,
    )
    proj = None
    for ref in (town_ref, tsib_ref):
        count = ref.shape[0] - rank - TAIL
        kernel_rows = quartic(product(ref[:count, :], pair), width).astype(jnp.bfloat16)
        term = product(ref[count:, :], kernel_rows)
        proj = term if proj is None else proj + term
    sums = sum(product(member, part, ((1,), (1,))) for part in thirds(proj))
    size = jnp.sum(member.astype(jnp.float32), axis=1, keepdims=True)
    sums = sums * (1.0 / jnp.maximum(size, 1.0))
    lane = lax.broadcasted_iota(jnp.int32, (SPB, TAIL), 1)
    means = jnp.zeros((SPB, TAIL), jnp.float32)
    for c in range(chips):
        means = jnp.where(lane == c, sums[c * SPB : (c + 1) * SPB, rank:], means)
    means = jnp.concatenate([means, jnp.zeros((SPB, rank - TAIL), jnp.float32)], axis=1)
    total = jnp.concatenate([sums[:, :rank], means], axis=0)
    if first:
        rest[0][...] = total
    else:
        rest[1][...] = rest[0][...] + total


def prior_part(masks, chips, width, first, own_ref, sib_ref, *rest):
    refs, rest = rest[: len(masks)], rest[len(masks) :]
    me = lax.axis_index("train")
    chip, core = me // 2, me % 2
    mine = jnp.concatenate([own_ref[:width, :], sib_ref[:width, :]], axis=1)
    none = jnp.zeros((SPB, own_ref.shape[1]), jnp.bfloat16)
    left = jnp.concatenate(
        [
            jnp.concatenate([member_of(own_ref, 0, SPB), none], axis=1),
            jnp.concatenate([none, member_of(sib_ref, 0, SPB)], axis=1),
        ],
        axis=0,
    )
    left_size = jnp.sum(left.astype(jnp.float32), axis=1, keepdims=True)
    total = None
    for i in range(0, len(masks), 2):
        two = refs[i : i + 2]
        pair = jnp.concatenate([ref[:width, :] for ref in two], axis=1)
        wide = jnp.concatenate(
            [
                member_of(ref, (lax.bitwise_xor(chip, mask) * 2 + core) * SPB, 2 * chips * SPB)
                for ref, mask in zip(two, masks[i : i + 2])
            ],
            axis=1,
        )
        wide_size = jnp.maximum(
            jnp.sum(wide.astype(jnp.float32), axis=1, keepdims=True), 1.0
        )
        pairs = quartic(product(mine, pair, ((0,), (0,))), width)
        half = sum(product(left, part) for part in thirds(pairs)) / left_size
        weight = thirds(wide.astype(jnp.float32) / wide_size)
        term = sum(
            product(a, b, ((1,), (1,)))
            for i, a in enumerate(thirds(half))
            for b in weight[: 3 - i]
        )
        total = term if total is None else total + term
    if first:
        rest[0][...] = total
    else:
        rest[1][...] = rest[0][...] + total


def finish(q_ref, other_ref, mine_ref, theirs_ref, mean_ref, cov_ref, all_ref):
    structs = q_ref.shape[0] - SPB
    me = lax.axis_index("train")
    chip, core = me // 2, me % 2
    for p in range(structs // SPB):
        rows = slice(p * SPB, (p + 1) * SPB)
        here = pl.multiple_of((2 * p + core) * SPB, SPB)
        there = pl.multiple_of((2 * p + 1 - core) * SPB, SPB)
        all_ref[pl.ds(here, SPB), :] = q_ref[rows, :]
        all_ref[pl.ds(there, SPB), :] = other_ref[rows, :]
    own = thirds(q_ref[pl.ds(pl.multiple_of(chip * SPB, SPB), SPB), :])
    every = thirds(all_ref[...])
    square = sum(
        product(a, b, ((1,), (1,))) for i, a in enumerate(own) for b in every[: 3 - i]
    )
    cov_ref[...] = mine_ref[...] + theirs_ref[...] - square
    lane = lax.broadcasted_iota(jnp.int32, (SPB, LANES), 1)
    row = lax.broadcasted_iota(jnp.int32, (SPB, LANES), 0)
    means = q_ref[structs:, :]
    column = jnp.sum(jnp.where(lane == chip, means, 0.0), axis=1, keepdims=True)
    mean_ref[...] = jnp.sum(jnp.where(lane == row, column, 0.0), axis=0)[:SPB]


def call(kernel, shapes, count, flops=0, scratch=()):
    many = isinstance(shapes, (tuple, list))
    return pl.pallas_call(
        kernel,
        out_shape=shapes,
        in_specs=[VMEM] * count,
        out_specs=[VMEM] * len(shapes) if many else VMEM,
        scratch_shapes=scratch,
        cost_estimate=pl.CostEstimate(flops=flops, bytes_accessed=0, transcendentals=0),
        compiler_params=pltpu.CompilerParams(vmem_limit_bytes=24 * 2**20),
    )


def body(size, cand_desc, struct_id, train_desc, lanczos, mean_weight):
    rows, width = cand_desc.shape
    count, rank = lanczos.shape
    chips = size // 2
    structs = chips * SPB

    def swap(value, mask):
        return lax.ppermute(value, "train", [(i, i ^ mask) for i in range(size)])

    block_shape = jax.ShapeDtypeStruct((width + TAIL, rows), jnp.bfloat16)
    own = pl.pallas_call(
        pack_cand,
        out_shape=block_shape,
        in_specs=[HBM, HBM],
        out_specs=VMEM,
        scratch_shapes=[
            pltpu.VMEM((rows, width), jnp.bfloat16),
            pltpu.VMEM((1, rows), jnp.int32),
            pltpu.SemaphoreType.DMA((2,)),
        ],
        compiler_params=pltpu.CompilerParams(vmem_limit_bytes=58 * 2**20),
    )(cand_desc, struct_id.reshape(1, rows))

    def again(value, other):
        return call(copy_after, block_shape, 2)(value, other)

    q_shape = jax.ShapeDtypeStruct((structs + SPB, rank), jnp.float32)
    prior_shape = jax.ShapeDtypeStruct((2 * SPB, 2 * structs), jnp.float32)

    def add_projection(masks, state, *pair):
        state = () if state is None else (state,)
        kernel = functools.partial(project, masks, chips, width, rank, not state)
        return call(
            kernel,
            q_shape,
            4 + len(state),
            flops=2 * 2 * rows * 2 * count * (width + 2 * rank),
        )(*pair, train_own, train_sib, *state)

    def add_prior(masks, state, *refs):
        state = () if state is None else (state,)
        kernel = functools.partial(prior_part, masks, chips, width, not state)
        return call(
            kernel,
            prior_shape,
            2 + len(refs) + len(state),
            flops=2 * 2 * rows * len(refs) * rows * (width + 2 * rank),
        )(own, sib, *refs, *state)

    train = (train_desc, lanczos, mean_weight)
    train_shape = jax.ShapeDtypeStruct((count + rank + TAIL, width), jnp.bfloat16)
    train_own, train_sib = call(pack_train, (train_shape, train_shape), 6)(
        *train, *[swap(value, 1) for value in train]
    )
    blocks = {0: own}
    if size == 16:
        for mask in (1, 4, 2):
            blocks[mask] = swap(own, 2 * mask)
        blocks[6] = swap(again(own, train_own), 12)
        blocks[3] = swap(blocks[2], 2)
        blocks[5] = swap(blocks[4], 2)
        blocks[7] = swap(blocks[6], 2)
    else:
        for mask in range(1, chips):
            blocks[mask] = swap(own, 2 * mask)
    sib = swap(own, 1)
    q = prior = None
    for mask in range(0, chips, 2):
        masks = (mask, mask + 1)
        q = add_projection(masks, q, blocks[mask], blocks[mask + 1])
    prior = add_prior(tuple(range(chips)), None, *[blocks[m] for m in range(chips)])

    theirs = swap(prior[SPB:], 1)
    mask = 2
    while mask < size:
        q = q + swap(q, mask)
        mask *= 2
    other = swap(q, 1)
    mean, covariance = call(
        finish,
        (
            jax.ShapeDtypeStruct((SPB,), jnp.float32),
            jax.ShapeDtypeStruct((SPB, 2 * structs), jnp.float32),
        ),
        4,
        scratch=[pltpu.VMEM((2 * structs, rank), jnp.float32)],
    )(q, other, prior[:SPB], theirs)
    return mean, covariance[None]


def solution(mesh):
    placed = (
        P(("pool", "cand", "train"), None),
        P(("pool", "cand", "train")),
        P(("pool", "train"), None),
        P(("pool", "train"), None),
        P(("pool", "train")),
    )
    return jax.shard_map(
        functools.partial(body, mesh.shape["train"]),
        mesh=mesh,
        in_specs=placed,
        out_specs=(P(("pool", "cand", "train")), P(("pool", "cand"), "train", None)),
        check_vma=False,
    )
```

```python
import functools

import jax
import jax.numpy as jnp
from jax import lax
from jax.experimental import pallas as pl
from jax.experimental.pallas import tpu as pltpu
from jax.sharding import PartitionSpec as P

SPB = 8
EPSILON = 1e-06
LANES = 128
TAIL = 16
VMEM = pl.BlockSpec(memory_space=pltpu.VMEM)
HBM = pl.BlockSpec(memory_space=pltpu.HBM)


def unit_rows(values):
    wide = values.astype(jnp.float32)
    scale = lax.rsqrt(jnp.mean(wide * wide, axis=1, keepdims=True) + EPSILON)
    return (wide * scale).astype(jnp.bfloat16)


def product(left, right, dims=((1,), (0,))):
    return lax.dot_general(
        left, right, (dims, ((), ())), preferred_element_type=jnp.float32
    )


def thirds(value):
    parts = []
    for _ in range(3):
        part = value.astype(jnp.bfloat16)
        parts.append(part)
        value = value - part.astype(jnp.float32)
    return parts


def pack_cand(cand_ref, ids_ref, out_ref, raw, ids, sems):
    rows, width = raw.shape
    copies = [
        pltpu.make_async_copy(cand_ref, raw, sems.at[0]),
        pltpu.make_async_copy(ids_ref, ids, sems.at[1]),
    ]
    for copy in copies:
        copy.start()
    for copy in copies:
        copy.wait()
    out_ref[:width, :] = unit_rows(raw[...]).T
    within = (ids[...] - ids[0, 0]).astype(jnp.float32)
    out_ref[width:, :] = jnp.broadcast_to(within, (TAIL, rows)).astype(jnp.bfloat16)


def pack_train(*refs):
    for train_ref, lanczos_ref, weight_ref, out_ref in (
        refs[:3] + refs[6:7],
        refs[3:6] + refs[7:],
    ):
        count, rank = lanczos_ref.shape
        step = count // 6
        for i in range(6):
            part = slice(i * step, (i + 1) * step)
            out_ref[part, :] = unit_rows(train_ref[part, :])
        out_ref[count : count + rank, :] = lanczos_ref[...].T
        out_ref[count + rank :, :] = jnp.broadcast_to(
            weight_ref[...].astype(jnp.float32).reshape(1, count), (TAIL, count)
        ).astype(jnp.bfloat16)


def copy_after(value_ref, _, *out_refs):
    start = 0
    for ref in out_refs:
        ref[...] = value_ref[start : start + ref.shape[0], :]
        start += ref.shape[0]


def quartic(products, width):
    cosine = products * (1.0 / width)
    square = cosine * cosine
    return square * square


def member_of(ref, base, count):
    ids = ref[ref.shape[0] - TAIL :, :][:1].astype(jnp.int32) + base
    row = lax.broadcasted_iota(jnp.int32, (count, ids.shape[1]), 0)
    return (row == ids).astype(jnp.bfloat16)


def project(masks, chips, width, rank, first, parts, *rest):
    refs, (town_ref, tsib_ref, *rest) = rest[: 2 * parts], rest[2 * parts :]
    chip = lax.axis_index("train") // 2
    one, two = (
        jnp.concatenate([ref[...] for ref in refs[i : i + parts]], axis=0)
        for i in (0, parts)
    )
    pair = jnp.concatenate([one[:width, :], two[:width, :]], axis=1)
    structs = chips * SPB
    member = jnp.concatenate(
        [
            member_of(ref, lax.bitwise_xor(chip, mask) * SPB, structs)
            for ref, mask in zip((one, two), masks)
        ],
        axis=1,
    )
    proj = None
    for ref in (town_ref, tsib_ref):
        count = ref.shape[0] - rank - TAIL
        kernel_rows = quartic(product(ref[:count, :], pair), width).astype(jnp.bfloat16)
        term = product(ref[count:, :], kernel_rows)
        proj = term if proj is None else proj + term
    sums = sum(product(member, part, ((1,), (1,))) for part in thirds(proj))
    size = jnp.sum(member.astype(jnp.float32), axis=1, keepdims=True)
    sums = sums * (1.0 / jnp.maximum(size, 1.0))
    lane = lax.broadcasted_iota(jnp.int32, (SPB, TAIL), 1)
    means = jnp.zeros((SPB, TAIL), jnp.float32)
    for c in range(chips):
        means = jnp.where(lane == c, sums[c * SPB : (c + 1) * SPB, rank:], means)
    means = jnp.concatenate([means, jnp.zeros((SPB, rank - TAIL), jnp.float32)], axis=1)
    total = jnp.concatenate([sums[:, :rank], means], axis=0)
    if first:
        rest[0][...] = total
    else:
        rest[1][...] = rest[0][...] + total


def prior_part(masks, chips, width, first, cuts, own_ref, sib_ref, *rest):
    refs = []
    for cut in cuts:
        refs.append(jnp.concatenate([ref[...] for ref in rest[:cut]], axis=0))
        rest = rest[cut:]
    me = lax.axis_index("train")
    chip, core = me // 2, me % 2
    mine = jnp.concatenate([own_ref[:width, :], sib_ref[:width, :]], axis=1)
    none = jnp.zeros((SPB, own_ref.shape[1]), jnp.bfloat16)
    left = jnp.concatenate(
        [
            jnp.concatenate([member_of(own_ref, 0, SPB), none], axis=1),
            jnp.concatenate([none, member_of(sib_ref, 0, SPB)], axis=1),
        ],
        axis=0,
    )
    left_size = jnp.sum(left.astype(jnp.float32), axis=1, keepdims=True)
    total = None
    for i in range(0, len(masks), 2):
        two = refs[i : i + 2]
        pair = jnp.concatenate([ref[:width, :] for ref in two], axis=1)
        wide = jnp.concatenate(
            [
                member_of(ref, (lax.bitwise_xor(chip, mask) * 2 + core) * SPB, 2 * chips * SPB)
                for ref, mask in zip(two, masks[i : i + 2])
            ],
            axis=1,
        )
        wide_size = jnp.maximum(
            jnp.sum(wide.astype(jnp.float32), axis=1, keepdims=True), 1.0
        )
        pairs = quartic(product(mine, pair, ((0,), (0,))), width)
        half = sum(product(left, part) for part in thirds(pairs)) / left_size
        weight = thirds(wide.astype(jnp.float32) / wide_size)
        term = sum(
            product(a, b, ((1,), (1,)))
            for i, a in enumerate(thirds(half))
            for b in weight[: 3 - i]
        )
        total = term if total is None else total + term
    if first:
        rest[0][...] = total
    else:
        rest[1][...] = rest[0][...] + total


def finish(q_ref, other_ref, mine_ref, theirs_ref, mean_ref, cov_ref, all_ref):
    structs = q_ref.shape[0] - SPB
    me = lax.axis_index("train")
    chip, core = me // 2, me % 2
    for p in range(structs // SPB):
        rows = slice(p * SPB, (p + 1) * SPB)
        here = pl.multiple_of((2 * p + core) * SPB, SPB)
        there = pl.multiple_of((2 * p + 1 - core) * SPB, SPB)
        all_ref[pl.ds(here, SPB), :] = q_ref[rows, :]
        all_ref[pl.ds(there, SPB), :] = other_ref[rows, :]
    own = thirds(q_ref[pl.ds(pl.multiple_of(chip * SPB, SPB), SPB), :])
    every = thirds(all_ref[...])
    square = sum(
        product(a, b, ((1,), (1,))) for i, a in enumerate(own) for b in every[: 3 - i]
    )
    cov_ref[...] = mine_ref[...] + theirs_ref[...] - square
    lane = lax.broadcasted_iota(jnp.int32, (SPB, LANES), 1)
    row = lax.broadcasted_iota(jnp.int32, (SPB, LANES), 0)
    means = q_ref[structs:, :]
    column = jnp.sum(jnp.where(lane == chip, means, 0.0), axis=1, keepdims=True)
    mean_ref[...] = jnp.sum(jnp.where(lane == row, column, 0.0), axis=0)[:SPB]


def call(kernel, shapes, count, flops=0, scratch=()):
    many = isinstance(shapes, (tuple, list))
    return pl.pallas_call(
        kernel,
        out_shape=shapes,
        in_specs=[VMEM] * count,
        out_specs=[VMEM] * len(shapes) if many else VMEM,
        scratch_shapes=scratch,
        cost_estimate=pl.CostEstimate(flops=flops, bytes_accessed=0, transcendentals=0),
        compiler_params=pltpu.CompilerParams(vmem_limit_bytes=24 * 2**20),
    )


def body(size, cand_desc, struct_id, train_desc, lanczos, mean_weight):
    rows, width = cand_desc.shape
    count, rank = lanczos.shape
    chips = size // 2
    structs = chips * SPB

    def swap(value, mask):
        return lax.ppermute(value, "train", [(i, i ^ mask) for i in range(size)])

    block_shape = jax.ShapeDtypeStruct((width + TAIL, rows), jnp.bfloat16)
    own = pl.pallas_call(
        pack_cand,
        out_shape=block_shape,
        in_specs=[HBM, HBM],
        out_specs=VMEM,
        scratch_shapes=[
            pltpu.VMEM((rows, width), jnp.bfloat16),
            pltpu.VMEM((1, rows), jnp.int32),
            pltpu.SemaphoreType.DMA((2,)),
        ],
        compiler_params=pltpu.CompilerParams(vmem_limit_bytes=58 * 2**20),
    )(cand_desc, struct_id.reshape(1, rows))

    def again(value, other, pieces):
        shapes = [
            jax.ShapeDtypeStruct((piece, value.shape[1]), value.dtype) for piece in pieces
        ]
        return pl.pallas_call(
            copy_after,
            out_shape=shapes,
            in_specs=[VMEM, pl.BlockSpec(memory_space=pl.ANY)],
            out_specs=[VMEM] * len(shapes),
            compiler_params=pltpu.CompilerParams(vmem_limit_bytes=24 * 2**20),
        )(value, other)

    def again_last(value, *others):
        return pl.pallas_call(
            lambda *refs: copy_after(refs[-2], None, refs[-1]),
            out_shape=block_shape,
            in_specs=[pl.BlockSpec(memory_space=pl.ANY)] * len(others) + [VMEM],
            out_specs=VMEM,
            compiler_params=pltpu.CompilerParams(vmem_limit_bytes=24 * 2**20),
        )(*others, value)

    def again_first(value, *others):
        return pl.pallas_call(
            lambda *refs: copy_after(refs[0], None, refs[-1]),
            out_shape=block_shape,
            in_specs=[VMEM] + [pl.BlockSpec(memory_space=pl.ANY)] * len(others),
            out_specs=VMEM,
            compiler_params=pltpu.CompilerParams(vmem_limit_bytes=24 * 2**20),
        )(value, *others)

    q_shape = jax.ShapeDtypeStruct((structs + SPB, rank), jnp.float32)
    prior_shape = jax.ShapeDtypeStruct((2 * SPB, 2 * structs), jnp.float32)

    def add_projection(masks, state, *pair):
        state = () if state is None else (state,)
        parts = len(pair) // 2
        kernel = functools.partial(project, masks, chips, width, rank, not state, parts)
        return call(
            kernel,
            q_shape,
            2 + len(pair) + len(state),
            flops=2 * 2 * rows * 2 * count * (width + 2 * rank),
        )(*pair, train_own, train_sib, *state)

    def add_prior(masks, state, *refs):
        state = () if state is None else (state,)
        cuts = tuple(len(ref) for ref in refs)
        refs = [part for ref in refs for part in ref]
        kernel = functools.partial(prior_part, masks, chips, width, not state, cuts)
        return call(
            kernel,
            prior_shape,
            2 + len(refs) + len(state),
            flops=2 * 2 * rows * len(refs) * rows * (width + 2 * rank),
        )(own, sib, *refs, *state)

    blocks = {0: own}
    if size == 16:
        for mask in (4, 1, 2):
            blocks[mask] = swap(own, 2 * mask)
    else:
        for mask in range(1, chips):
            blocks[mask] = swap(own, 2 * mask)
    train = (train_desc, lanczos, mean_weight)
    train_shape = jax.ShapeDtypeStruct((count + rank + TAIL, width), jnp.bfloat16)
    train_own, train_sib = call(pack_train, (train_shape, train_shape), 6)(
        *train, *[swap(value, 1) for value in train]
    )
    if size == 16:
        far = again_first(blocks[4], blocks[1], blocks[2], train_own)
        blocks[6] = swap(far, 4)
        blocks[5] = swap(far, 2)
        blocks[3] = swap(blocks[1], 4)
        blocks[7] = swap(blocks[6], 2)
    blocks = {m: b if isinstance(b, (tuple, list)) else (b,) for m, b in blocks.items()}
    sib = swap(own, 1)
    q = prior = None
    groups = [(m, m + 1) for m in range(0, chips, 2)]
    if size == 16:
        groups = [(0, 1), (4, 5), (2, 6), (3, 7)]
    for masks in groups:
        q = add_projection(masks, q, *blocks[masks[0]], *blocks[masks[1]])
    prior = add_prior(tuple(range(chips)), None, *[blocks[m] for m in range(chips)])

    theirs = swap(prior[SPB:], 1)
    mask = 2
    while mask < size:
        q = q + swap(q, mask)
        mask *= 2
    other = swap(q, 1)
    mean, covariance = call(
        finish,
        (
            jax.ShapeDtypeStruct((SPB,), jnp.float32),
            jax.ShapeDtypeStruct((SPB, 2 * structs), jnp.float32),
        ),
        4,
        scratch=[pltpu.VMEM((2 * structs, rank), jnp.float32)],
    )(q, other, prior[:SPB], theirs)
    return mean, covariance[None]


def solution(mesh):
    placed = (
        P(("pool", "cand", "train"), None),
        P(("pool", "cand", "train")),
        P(("pool", "train"), None),
        P(("pool", "train"), None),
        P(("pool", "train")),
    )
    return jax.shard_map(
        functools.partial(body, mesh.shape["train"]),
        mesh=mesh,
        in_specs=placed,
        out_specs=(P(("pool", "cand", "train")), P(("pool", "cand"), "train", None)),
        check_vma=False,
    )
```

```python
import functools

import jax
import jax.numpy as jnp
from jax import lax
from jax.experimental import pallas as pl
from jax.experimental.pallas import tpu as pltpu
from jax.sharding import PartitionSpec as P

SPB = 8
EPSILON = 1e-06
LANES = 128
TAIL = 16
VMEM = pl.BlockSpec(memory_space=pltpu.VMEM)
HBM = pl.BlockSpec(memory_space=pltpu.HBM)


def unit_rows(values):
    wide = values.astype(jnp.float32)
    scale = lax.rsqrt(jnp.mean(wide * wide, axis=1, keepdims=True) + EPSILON)
    return (wide * scale).astype(jnp.bfloat16)


def product(left, right, dims=((1,), (0,))):
    return lax.dot_general(
        left, right, (dims, ((), ())), preferred_element_type=jnp.float32
    )


def thirds(value):
    parts = []
    for _ in range(3):
        part = value.astype(jnp.bfloat16)
        parts.append(part)
        value = value - part.astype(jnp.float32)
    return parts


def pack_cand(cand_ref, ids_ref, out_ref, raw, ids, sems):
    rows, width = raw.shape
    copies = [
        pltpu.make_async_copy(cand_ref, raw, sems.at[0]),
        pltpu.make_async_copy(ids_ref, ids, sems.at[1]),
    ]
    for copy in copies:
        copy.start()
    for copy in copies:
        copy.wait()
    out_ref[:width, :] = unit_rows(raw[...]).T
    within = (ids[...] - ids[0, 0]).astype(jnp.float32)
    out_ref[width:, :] = jnp.broadcast_to(within, (TAIL, rows)).astype(jnp.bfloat16)


def pack_train(*refs):
    for train_ref, lanczos_ref, weight_ref, out_ref in (
        refs[:3] + refs[6:7],
        refs[3:6] + refs[7:],
    ):
        count, rank = lanczos_ref.shape
        step = count // 6
        for i in range(6):
            part = slice(i * step, (i + 1) * step)
            out_ref[part, :] = unit_rows(train_ref[part, :])
        out_ref[count : count + rank, :] = lanczos_ref[...].T
        out_ref[count + rank :, :] = jnp.broadcast_to(
            weight_ref[...].astype(jnp.float32).reshape(1, count), (TAIL, count)
        ).astype(jnp.bfloat16)


def copy_after(value_ref, _, *out_refs):
    start = 0
    for ref in out_refs:
        ref[...] = value_ref[start : start + ref.shape[0], :]
        start += ref.shape[0]


def quartic(products, width):
    cosine = products * (1.0 / width)
    square = cosine * cosine
    return square * square


def member_of(ref, base, count):
    ids = ref[ref.shape[0] - TAIL :, :][:1].astype(jnp.int32) + base
    row = lax.broadcasted_iota(jnp.int32, (count, ids.shape[1]), 0)
    return (row == ids).astype(jnp.bfloat16)


def project(masks, chips, width, rank, first, cut, parts, *rest):
    refs, (town_ref, tsib_ref, *rest) = rest[:parts], rest[parts:]
    chip = lax.axis_index("train") // 2
    one, two = (
        jnp.concatenate([ref[...] for ref in piece], axis=0)
        for piece in (refs[:cut], refs[cut:])
    )
    pair = jnp.concatenate([one[:width, :], two[:width, :]], axis=1)
    structs = chips * SPB
    member = jnp.concatenate(
        [
            member_of(ref, lax.bitwise_xor(chip, mask) * SPB, structs)
            for ref, mask in zip((one, two), masks)
        ],
        axis=1,
    )
    proj = None
    for ref in (town_ref, tsib_ref):
        count = ref.shape[0] - rank - TAIL
        kernel_rows = quartic(product(ref[:count, :], pair), width).astype(jnp.bfloat16)
        term = product(ref[count:, :], kernel_rows)
        proj = term if proj is None else proj + term
    sums = sum(product(member, part, ((1,), (1,))) for part in thirds(proj))
    size = jnp.sum(member.astype(jnp.float32), axis=1, keepdims=True)
    sums = sums * (1.0 / jnp.maximum(size, 1.0))
    lane = lax.broadcasted_iota(jnp.int32, (SPB, TAIL), 1)
    means = jnp.zeros((SPB, TAIL), jnp.float32)
    for c in range(chips):
        means = jnp.where(lane == c, sums[c * SPB : (c + 1) * SPB, rank:], means)
    means = jnp.concatenate([means, jnp.zeros((SPB, rank - TAIL), jnp.float32)], axis=1)
    total = jnp.concatenate([sums[:, :rank], means], axis=0)
    if first:
        rest[0][...] = total
    else:
        rest[1][...] = rest[0][...] + total


def prior_part(masks, chips, width, first, cuts, own_ref, sib_ref, *rest):
    refs = []
    for cut in cuts:
        refs.append(jnp.concatenate([ref[...] for ref in rest[:cut]], axis=0))
        rest = rest[cut:]
    me = lax.axis_index("train")
    chip, core = me // 2, me % 2
    mine = jnp.concatenate([own_ref[:width, :], sib_ref[:width, :]], axis=1)
    none = jnp.zeros((SPB, own_ref.shape[1]), jnp.bfloat16)
    left = jnp.concatenate(
        [
            jnp.concatenate([member_of(own_ref, 0, SPB), none], axis=1),
            jnp.concatenate([none, member_of(sib_ref, 0, SPB)], axis=1),
        ],
        axis=0,
    )
    left_size = jnp.sum(left.astype(jnp.float32), axis=1, keepdims=True)
    total = None
    for i in range(0, len(masks), 2):
        two = refs[i : i + 2]
        pair = jnp.concatenate([ref[:width, :] for ref in two], axis=1)
        wide = jnp.concatenate(
            [
                member_of(ref, (lax.bitwise_xor(chip, mask) * 2 + core) * SPB, 2 * chips * SPB)
                for ref, mask in zip(two, masks[i : i + 2])
            ],
            axis=1,
        )
        wide_size = jnp.maximum(
            jnp.sum(wide.astype(jnp.float32), axis=1, keepdims=True), 1.0
        )
        pairs = quartic(product(mine, pair, ((0,), (0,))), width)
        half = sum(product(left, part) for part in thirds(pairs)) / left_size
        weight = thirds(wide.astype(jnp.float32) / wide_size)
        term = sum(
            product(a, b, ((1,), (1,)))
            for i, a in enumerate(thirds(half))
            for b in weight[: 3 - i]
        )
        total = term if total is None else total + term
    if first:
        rest[0][...] = total
    else:
        rest[1][...] = rest[0][...] + total


def last_sum(q_ref, more_ref, prior_ref, out_ref):
    rows = q_ref.shape[0]
    out_ref[:rows, :] = q_ref[...] + more_ref[...]
    for i in range(prior_ref.shape[1] // LANES):
        out_ref[rows + i * SPB : rows + (i + 1) * SPB, :] = prior_ref[
            SPB:, i * LANES : (i + 1) * LANES
        ]


def finish(q_ref, other_ref, prior_ref, mean_ref, cov_ref, all_ref):
    wide = prior_ref.shape[1]
    structs = wide // 2
    me = lax.axis_index("train")
    chip, core = me // 2, me % 2
    for p in range(structs // SPB):
        rows = slice(p * SPB, (p + 1) * SPB)
        here = pl.multiple_of((2 * p + core) * SPB, SPB)
        there = pl.multiple_of((2 * p + 1 - core) * SPB, SPB)
        all_ref[pl.ds(here, SPB), :] = q_ref[rows, :]
        all_ref[pl.ds(there, SPB), :] = other_ref[rows, :]
    own = thirds(q_ref[pl.ds(pl.multiple_of(chip * SPB, SPB), SPB), :])
    every = thirds(all_ref[...])
    square = sum(
        product(a, b, ((1,), (1,))) for i, a in enumerate(own) for b in every[: 3 - i]
    )
    start = structs + SPB
    theirs = [
        other_ref[start + i * SPB : start + (i + 1) * SPB, :] for i in range(wide // LANES)
    ]
    cov_ref[...] = prior_ref[:SPB, :] + jnp.concatenate(theirs, axis=1) - square
    lane = lax.broadcasted_iota(jnp.int32, (SPB, LANES), 1)
    row = lax.broadcasted_iota(jnp.int32, (SPB, LANES), 0)
    means = q_ref[structs:start, :]
    column = jnp.sum(jnp.where(lane == chip, means, 0.0), axis=1, keepdims=True)
    mean_ref[...] = jnp.sum(jnp.where(lane == row, column, 0.0), axis=0)[:SPB]


def call(kernel, shapes, count, flops=0, scratch=()):
    many = isinstance(shapes, (tuple, list))
    return pl.pallas_call(
        kernel,
        out_shape=shapes,
        in_specs=[VMEM] * count,
        out_specs=[VMEM] * len(shapes) if many else VMEM,
        scratch_shapes=scratch,
        cost_estimate=pl.CostEstimate(flops=flops, bytes_accessed=0, transcendentals=0),
        compiler_params=pltpu.CompilerParams(vmem_limit_bytes=24 * 2**20),
    )


def body(size, cand_desc, struct_id, train_desc, lanczos, mean_weight):
    rows, width = cand_desc.shape
    count, rank = lanczos.shape
    chips = size // 2
    structs = chips * SPB

    def swap(value, mask):
        return lax.ppermute(value, "train", [(i, i ^ mask) for i in range(size)])

    block_shape = jax.ShapeDtypeStruct((width + TAIL, rows), jnp.bfloat16)
    own = pl.pallas_call(
        pack_cand,
        out_shape=block_shape,
        in_specs=[HBM, HBM],
        out_specs=VMEM,
        scratch_shapes=[
            pltpu.VMEM((rows, width), jnp.bfloat16),
            pltpu.VMEM((1, rows), jnp.int32),
            pltpu.SemaphoreType.DMA((2,)),
        ],
        compiler_params=pltpu.CompilerParams(vmem_limit_bytes=58 * 2**20),
    )(cand_desc, struct_id.reshape(1, rows))

    def again(value, other, pieces):
        shapes = [
            jax.ShapeDtypeStruct((piece, value.shape[1]), value.dtype) for piece in pieces
        ]
        return pl.pallas_call(
            copy_after,
            out_shape=shapes,
            in_specs=[VMEM, pl.BlockSpec(memory_space=pl.ANY)],
            out_specs=[VMEM] * len(shapes),
            compiler_params=pltpu.CompilerParams(vmem_limit_bytes=24 * 2**20),
        )(value, other)

    def again_last(value, *others):
        return pl.pallas_call(
            lambda *refs: copy_after(refs[-2], None, refs[-1]),
            out_shape=block_shape,
            in_specs=[pl.BlockSpec(memory_space=pl.ANY)] * len(others) + [VMEM],
            out_specs=VMEM,
            compiler_params=pltpu.CompilerParams(vmem_limit_bytes=24 * 2**20),
        )(*others, value)

    def again_pieces(value, pieces, *others):
        shapes = [
            jax.ShapeDtypeStruct((piece, value.shape[1]), value.dtype) for piece in pieces
        ]
        def kernel(*refs):
            refs[1 + len(others)][...] = refs[0][...]
            copy_after(refs[0], None, *refs[2 + len(others) :])
        return pl.pallas_call(
            kernel,
            out_shape=[block_shape, *shapes],
            in_specs=[VMEM] + [pl.BlockSpec(memory_space=pl.ANY)] * len(others),
            out_specs=[VMEM] * (1 + len(shapes)),
            compiler_params=pltpu.CompilerParams(vmem_limit_bytes=24 * 2**20),
        )(value, *others)

    def again_first(value, *others):
        return pl.pallas_call(
            lambda *refs: copy_after(refs[0], None, refs[-1]),
            out_shape=block_shape,
            in_specs=[VMEM] + [pl.BlockSpec(memory_space=pl.ANY)] * len(others),
            out_specs=VMEM,
            compiler_params=pltpu.CompilerParams(vmem_limit_bytes=24 * 2**20),
        )(value, *others)

    q_shape = jax.ShapeDtypeStruct((structs + SPB, rank), jnp.float32)
    prior_shape = jax.ShapeDtypeStruct((2 * SPB, 2 * structs), jnp.float32)

    def add_projection(masks, state, one, two):
        state = () if state is None else (state,)
        pair = (*one, *two)
        kernel = functools.partial(
            project, masks, chips, width, rank, not state, len(one), len(pair)
        )
        return call(
            kernel,
            q_shape,
            2 + len(pair) + len(state),
            flops=2 * 2 * rows * 2 * count * (width + 2 * rank),
        )(*pair, train_own, train_sib, *state)

    def add_prior(masks, state, *refs):
        state = () if state is None else (state,)
        cuts = tuple(len(ref) for ref in refs)
        refs = [part for ref in refs for part in ref]
        kernel = functools.partial(prior_part, masks, chips, width, not state, cuts)
        return call(
            kernel,
            prior_shape,
            2 + len(refs) + len(state),
            flops=2 * 2 * rows * len(refs) * rows * (width + 2 * rank),
        )(own, sib, *refs, *state)

    blocks = {0: own}
    if size == 16:
        for mask in (2, 4, 1):
            blocks[mask] = swap(own, 2 * mask)
    else:
        for mask in range(1, chips):
            blocks[mask] = swap(own, 2 * mask)
    train = (train_desc, lanczos, mean_weight)
    train_shape = jax.ShapeDtypeStruct((count + rank + TAIL, width), jnp.bfloat16)
    train_own, train_sib = call(pack_train, (train_shape, train_shape), 6)(
        *train, *[swap(value, 1) for value in train]
    )
    if size == 16:
        far = again_first(blocks[4], blocks[2], train_own)
        blocks[6] = swap(far, 4)
        blocks[5] = swap(far, 2)
        blocks[3] = swap(blocks[1], 4)
        blocks[7] = swap(blocks[6], 2)
        groups = ((0, 1), (2, 4), (5, 6), (3, 7))
    else:
        groups = [(m, m + 1) for m in range(0, chips, 2)]
    blocks = {m: b if isinstance(b, (tuple, list)) else (b,) for m, b in blocks.items()}
    q = None
    for one, two in groups:
        q = add_projection((one, two), q, blocks[one], blocks[two])
    sib = swap(own, 1)
    prior = add_prior(tuple(range(chips)), None, *[blocks[m] for m in range(chips)])

    mask = 2
    while mask < size // 2:
        q = q + swap(q, mask)
        mask *= 2
    tail = structs + SPB + 2 * structs // LANES * SPB
    q = call(last_sum, jax.ShapeDtypeStruct((tail, rank), jnp.float32), 3)(
        q, swap(q, mask), prior
    )
    mean, covariance = call(
        finish,
        (
            jax.ShapeDtypeStruct((SPB,), jnp.float32),
            jax.ShapeDtypeStruct((SPB, 2 * structs), jnp.float32),
        ),
        3,
        scratch=[pltpu.VMEM((2 * structs, rank), jnp.float32)],
    )(q, swap(q, 1), prior)
    return mean, covariance[None]


def solution(mesh):
    placed = (
        P(("pool", "cand", "train"), None),
        P(("pool", "cand", "train")),
        P(("pool", "train"), None),
        P(("pool", "train"), None),
        P(("pool", "train")),
    )
    return jax.shard_map(
        functools.partial(body, mesh.shape["train"]),
        mesh=mesh,
        in_specs=placed,
        out_specs=(P(("pool", "cand", "train")), P(("pool", "cand"), "train", None)),
        check_vma=False,
    )
```

```python
import functools

import jax
import jax.numpy as jnp
from jax import lax
from jax.experimental import pallas as pl
from jax.experimental.pallas import tpu as pltpu
from jax.sharding import PartitionSpec as P

SPB = 8
EPSILON = 1e-06
LANES = 128
TAIL = 16
VMEM = pl.BlockSpec(memory_space=pltpu.VMEM)
HBM = pl.BlockSpec(memory_space=pltpu.HBM)


def unit_rows(values):
    wide = values.astype(jnp.float32)
    scale = lax.rsqrt(jnp.mean(wide * wide, axis=1, keepdims=True) + EPSILON)
    return (wide * scale).astype(jnp.bfloat16)


def product(left, right, dims=((1,), (0,))):
    return lax.dot_general(
        left, right, (dims, ((), ())), preferred_element_type=jnp.float32
    )


def thirds(value):
    parts = []
    for _ in range(3):
        part = value.astype(jnp.bfloat16)
        parts.append(part)
        value = value - part.astype(jnp.float32)
    return parts


def pack_cand(cand_ref, ids_ref, out_ref, raw, ids, sems):
    rows, width = raw.shape
    copies = [
        pltpu.make_async_copy(cand_ref, raw, sems.at[0]),
        pltpu.make_async_copy(ids_ref, ids, sems.at[1]),
    ]
    for copy in copies:
        copy.start()
    for copy in copies:
        copy.wait()
    out_ref[:width, :] = unit_rows(raw[...]).T
    within = (ids[...] - ids[0, 0]).astype(jnp.float32)
    out_ref[width:, :] = jnp.broadcast_to(within, (TAIL, rows)).astype(jnp.bfloat16)


def pack_here(cand_ref, ids_ref, *rest):
    out_ref = rest[-1]
    rows, width = cand_ref.shape
    out_ref[:width, :] = unit_rows(cand_ref[...]).T
    within = (ids_ref[...] - ids_ref[0, 0]).astype(jnp.float32)
    out_ref[width:, :] = jnp.broadcast_to(within, (TAIL, rows)).astype(jnp.bfloat16)


def pack_train(*refs):
    for train_ref, lanczos_ref, weight_ref, out_ref in (
        refs[:3] + refs[6:7],
        refs[3:6] + refs[7:],
    ):
        count, rank = lanczos_ref.shape
        step = count // 6
        for i in range(6):
            part = slice(i * step, (i + 1) * step)
            out_ref[part, :] = unit_rows(train_ref[part, :])
        out_ref[count : count + rank, :] = lanczos_ref[...].T
        out_ref[count + rank :, :] = jnp.broadcast_to(
            weight_ref[...].astype(jnp.float32).reshape(1, count), (TAIL, count)
        ).astype(jnp.bfloat16)


def copy_after(value_ref, _, *out_refs):
    start = 0
    for ref in out_refs:
        ref[...] = value_ref[start : start + ref.shape[0], :]
        start += ref.shape[0]


def quartic(products, width):
    cosine = products * (1.0 / width)
    square = cosine * cosine
    return square * square


def member_of(ref, base, count):
    ids = ref[ref.shape[0] - TAIL :, :][:1].astype(jnp.int32) + base
    row = lax.broadcasted_iota(jnp.int32, (count, ids.shape[1]), 0)
    return (row == ids).astype(jnp.bfloat16)


def project(masks, chips, width, rank, first, cut, parts, *rest):
    refs, (town_ref, tsib_ref, *rest) = rest[:parts], rest[parts:]
    chip = lax.axis_index("train") // 2
    one, two = (
        jnp.concatenate([ref[...] for ref in piece], axis=0)
        for piece in (refs[:cut], refs[cut:])
    )
    pair = jnp.concatenate([one[:width, :], two[:width, :]], axis=1)
    structs = chips * SPB
    member = jnp.concatenate(
        [
            member_of(ref, lax.bitwise_xor(chip, mask) * SPB, structs)
            for ref, mask in zip((one, two), masks)
        ],
        axis=1,
    )
    proj = None
    for ref in (town_ref, tsib_ref):
        count = ref.shape[0] - rank - TAIL
        kernel_rows = quartic(product(ref[:count, :], pair), width).astype(jnp.bfloat16)
        term = product(ref[count:, :], kernel_rows)
        proj = term if proj is None else proj + term
    sums = sum(product(member, part, ((1,), (1,))) for part in thirds(proj))
    size = jnp.sum(member.astype(jnp.float32), axis=1, keepdims=True)
    sums = sums * (1.0 / jnp.maximum(size, 1.0))
    lane = lax.broadcasted_iota(jnp.int32, (SPB, TAIL), 1)
    means = jnp.zeros((SPB, TAIL), jnp.float32)
    for c in range(chips):
        means = jnp.where(lane == c, sums[c * SPB : (c + 1) * SPB, rank:], means)
    means = jnp.concatenate([means, jnp.zeros((SPB, rank - TAIL), jnp.float32)], axis=1)
    total = jnp.concatenate([sums[:, :rank], means], axis=0)
    if first:
        rest[0][...] = total
    else:
        rest[1][...] = rest[0][...] + total


def prior_part(masks, chips, width, first, cuts, own_ref, sib_ref, *rest):
    refs = []
    for cut in cuts:
        refs.append(jnp.concatenate([ref[...] for ref in rest[:cut]], axis=0))
        rest = rest[cut:]
    me = lax.axis_index("train")
    chip, core = me // 2, me % 2
    mine = jnp.concatenate([own_ref[:width, :], sib_ref[:width, :]], axis=1)
    none = jnp.zeros((SPB, own_ref.shape[1]), jnp.bfloat16)
    left = jnp.concatenate(
        [
            jnp.concatenate([member_of(own_ref, 0, SPB), none], axis=1),
            jnp.concatenate([none, member_of(sib_ref, 0, SPB)], axis=1),
        ],
        axis=0,
    )
    left_size = jnp.sum(left.astype(jnp.float32), axis=1, keepdims=True)
    total = None
    for i in range(0, len(masks), 2):
        two = refs[i : i + 2]
        pair = jnp.concatenate([ref[:width, :] for ref in two], axis=1)
        wide = jnp.concatenate(
            [
                member_of(ref, (lax.bitwise_xor(chip, mask) * 2 + core) * SPB, 2 * chips * SPB)
                for ref, mask in zip(two, masks[i : i + 2])
            ],
            axis=1,
        )
        wide_size = jnp.maximum(
            jnp.sum(wide.astype(jnp.float32), axis=1, keepdims=True), 1.0
        )
        pairs = quartic(product(mine, pair, ((0,), (0,))), width)
        half = sum(product(left, part) for part in thirds(pairs)) / left_size
        weight = thirds(wide.astype(jnp.float32) / wide_size)
        term = sum(
            product(a, b, ((1,), (1,)))
            for i, a in enumerate(thirds(half))
            for b in weight[: 3 - i]
        )
        total = term if total is None else total + term
    if first:
        rest[0][...] = total
    else:
        rest[1][...] = rest[0][...] + total


def last_sum(q_ref, more_ref, prior_ref, out_ref):
    rows = q_ref.shape[0]
    out_ref[:rows, :] = q_ref[...] + more_ref[...]
    for i in range(prior_ref.shape[1] // LANES):
        out_ref[rows + i * SPB : rows + (i + 1) * SPB, :] = prior_ref[
            SPB:, i * LANES : (i + 1) * LANES
        ]


def finish(q_ref, other_ref, prior_ref, mean_ref, cov_ref, all_ref):
    wide = prior_ref.shape[1]
    structs = wide // 2
    me = lax.axis_index("train")
    chip, core = me // 2, me % 2
    for p in range(structs // SPB):
        rows = slice(p * SPB, (p + 1) * SPB)
        here = pl.multiple_of((2 * p + core) * SPB, SPB)
        there = pl.multiple_of((2 * p + 1 - core) * SPB, SPB)
        all_ref[pl.ds(here, SPB), :] = q_ref[rows, :]
        all_ref[pl.ds(there, SPB), :] = other_ref[rows, :]
    own = thirds(q_ref[pl.ds(pl.multiple_of(chip * SPB, SPB), SPB), :])
    every = thirds(all_ref[...])
    square = sum(
        product(a, b, ((1,), (1,))) for i, a in enumerate(own) for b in every[: 3 - i]
    )
    start = structs + SPB
    theirs = [
        other_ref[start + i * SPB : start + (i + 1) * SPB, :] for i in range(wide // LANES)
    ]
    cov_ref[...] = prior_ref[:SPB, :] + jnp.concatenate(theirs, axis=1) - square
    lane = lax.broadcasted_iota(jnp.int32, (SPB, LANES), 1)
    row = lax.broadcasted_iota(jnp.int32, (SPB, LANES), 0)
    means = q_ref[structs:start, :]
    column = jnp.sum(jnp.where(lane == chip, means, 0.0), axis=1, keepdims=True)
    mean_ref[...] = jnp.sum(jnp.where(lane == row, column, 0.0), axis=0)[:SPB]


def call(kernel, shapes, count, flops=0, scratch=()):
    many = isinstance(shapes, (tuple, list))
    return pl.pallas_call(
        kernel,
        out_shape=shapes,
        in_specs=[VMEM] * count,
        out_specs=[VMEM] * len(shapes) if many else VMEM,
        scratch_shapes=scratch,
        cost_estimate=pl.CostEstimate(flops=flops, bytes_accessed=0, transcendentals=0),
        compiler_params=pltpu.CompilerParams(vmem_limit_bytes=24 * 2**20),
    )


def body(size, cand_desc, struct_id, train_desc, lanczos, mean_weight):
    rows, width = cand_desc.shape
    count, rank = lanczos.shape
    chips = size // 2
    structs = chips * SPB

    def swap(value, mask):
        return lax.ppermute(value, "train", [(i, i ^ mask) for i in range(size)])

    block_shape = jax.ShapeDtypeStruct((width + TAIL, rows), jnp.bfloat16)
    own = pl.pallas_call(
        pack_cand,
        out_shape=block_shape,
        in_specs=[HBM, HBM],
        out_specs=VMEM,
        scratch_shapes=[
            pltpu.VMEM((rows, width), jnp.bfloat16),
            pltpu.VMEM((1, rows), jnp.int32),
            pltpu.SemaphoreType.DMA((2,)),
        ],
        compiler_params=pltpu.CompilerParams(vmem_limit_bytes=58 * 2**20),
    )(cand_desc, struct_id.reshape(1, rows))

    def again(value, other, pieces):
        shapes = [
            jax.ShapeDtypeStruct((piece, value.shape[1]), value.dtype) for piece in pieces
        ]
        return pl.pallas_call(
            copy_after,
            out_shape=shapes,
            in_specs=[VMEM, pl.BlockSpec(memory_space=pl.ANY)],
            out_specs=[VMEM] * len(shapes),
            compiler_params=pltpu.CompilerParams(vmem_limit_bytes=24 * 2**20),
        )(value, other)

    def again_last(value, *others):
        return pl.pallas_call(
            lambda *refs: copy_after(refs[-2], None, refs[-1]),
            out_shape=block_shape,
            in_specs=[pl.BlockSpec(memory_space=pl.ANY)] * len(others) + [VMEM],
            out_specs=VMEM,
            compiler_params=pltpu.CompilerParams(vmem_limit_bytes=24 * 2**20),
        )(*others, value)

    def pack_received(mask, *others):
        return pl.pallas_call(
            pack_here,
            out_shape=block_shape,
            in_specs=[VMEM, VMEM] + [pl.BlockSpec(memory_space=pl.ANY)] * len(others),
            out_specs=VMEM,
            compiler_params=pltpu.CompilerParams(vmem_limit_bytes=24 * 2**20),
        )(swap(cand_desc, mask), swap(struct_id.reshape(1, rows), mask), *others)

    def again_pieces(value, pieces, *others):
        shapes = [
            jax.ShapeDtypeStruct((piece, value.shape[1]), value.dtype) for piece in pieces
        ]
        def kernel(*refs):
            refs[1 + len(others)][...] = refs[0][...]
            copy_after(refs[0], None, *refs[2 + len(others) :])
        return pl.pallas_call(
            kernel,
            out_shape=[block_shape, *shapes],
            in_specs=[VMEM] + [pl.BlockSpec(memory_space=pl.ANY)] * len(others),
            out_specs=[VMEM] * (1 + len(shapes)),
            compiler_params=pltpu.CompilerParams(vmem_limit_bytes=24 * 2**20),
        )(value, *others)

    def again_first(value, *others):
        return pl.pallas_call(
            lambda *refs: copy_after(refs[0], None, refs[-1]),
            out_shape=block_shape,
            in_specs=[VMEM] + [pl.BlockSpec(memory_space=pl.ANY)] * len(others),
            out_specs=VMEM,
            compiler_params=pltpu.CompilerParams(vmem_limit_bytes=24 * 2**20),
        )(value, *others)

    q_shape = jax.ShapeDtypeStruct((structs + SPB, rank), jnp.float32)
    prior_shape = jax.ShapeDtypeStruct((2 * SPB, 2 * structs), jnp.float32)

    def add_projection(masks, state, one, two):
        state = () if state is None else (state,)
        pair = (*one, *two)
        kernel = functools.partial(
            project, masks, chips, width, rank, not state, len(one), len(pair)
        )
        return call(
            kernel,
            q_shape,
            2 + len(pair) + len(state),
            flops=2 * 2 * rows * 2 * count * (width + 2 * rank),
        )(*pair, train_own, train_sib, *state)

    def add_prior(masks, state, *refs):
        state = () if state is None else (state,)
        cuts = tuple(len(ref) for ref in refs)
        refs = [part for ref in refs for part in ref]
        kernel = functools.partial(prior_part, masks, chips, width, not state, cuts)
        return call(
            kernel,
            prior_shape,
            2 + len(refs) + len(state),
            flops=2 * 2 * rows * len(refs) * rows * (width + 2 * rank),
        )(own, sib, *refs, *state)

    blocks = {0: own}
    if size == 16:
        for mask in (2, 1):
            blocks[mask] = swap(own, 2 * mask)
    else:
        for mask in range(1, chips):
            blocks[mask] = swap(own, 2 * mask)
    train = (train_desc, lanczos, mean_weight)
    train_shape = jax.ShapeDtypeStruct((count + rank + TAIL, width), jnp.bfloat16)
    train_own, train_sib = call(pack_train, (train_shape, train_shape), 6)(
        *train, *[swap(value, 1) for value in train]
    )
    if size == 16:
        far = pack_received(8, train_own)
        blocks[4] = far
        late = again_first(far, blocks[2])
        blocks[6] = swap(far, 4)
        blocks[5] = swap(late, 2)
        blocks[3] = swap(blocks[1], 4)
        blocks[7] = swap(blocks[6], 2)
        groups = ((0, 1), (2, 4), (5, 6), (3, 7))
    else:
        groups = [(m, m + 1) for m in range(0, chips, 2)]
    blocks = {m: b if isinstance(b, (tuple, list)) else (b,) for m, b in blocks.items()}
    q = None
    for one, two in groups:
        q = add_projection((one, two), q, blocks[one], blocks[two])
    sib = swap(own, 1)
    prior = add_prior(tuple(range(chips)), None, *[blocks[m] for m in range(chips)])

    mask = 2
    while mask < size // 2:
        q = q + swap(q, mask)
        mask *= 2
    tail = structs + SPB + 2 * structs // LANES * SPB
    q = call(last_sum, jax.ShapeDtypeStruct((tail, rank), jnp.float32), 3)(
        q, swap(q, mask), prior
    )
    mean, covariance = call(
        finish,
        (
            jax.ShapeDtypeStruct((SPB,), jnp.float32),
            jax.ShapeDtypeStruct((SPB, 2 * structs), jnp.float32),
        ),
        3,
        scratch=[pltpu.VMEM((2 * structs, rank), jnp.float32)],
    )(q, swap(q, 1), prior)
    return mean, covariance[None]


def solution(mesh):
    placed = (
        P(("pool", "cand", "train"), None),
        P(("pool", "cand", "train")),
        P(("pool", "train"), None),
        P(("pool", "train"), None),
        P(("pool", "train")),
    )
    return jax.shard_map(
        functools.partial(body, mesh.shape["train"]),
        mesh=mesh,
        in_specs=placed,
        out_specs=(P(("pool", "cand", "train")), P(("pool", "cand"), "train", None)),
        check_vma=False,
    )
```

```python
import functools

import jax
import jax.numpy as jnp
from jax import lax
from jax.experimental import pallas as pl
from jax.experimental.pallas import tpu as pltpu
from jax.sharding import PartitionSpec as P

SPB = 8
EPSILON = 1e-06
LANES = 128
TAIL = 16
VMEM = pl.BlockSpec(memory_space=pltpu.VMEM)
HBM = pl.BlockSpec(memory_space=pltpu.HBM)


def unit_rows(values):
    wide = values.astype(jnp.float32)
    scale = lax.rsqrt(jnp.mean(wide * wide, axis=1, keepdims=True) + EPSILON)
    return (wide * scale).astype(jnp.bfloat16)


def product(left, right, dims=((1,), (0,))):
    return lax.dot_general(
        left, right, (dims, ((), ())), preferred_element_type=jnp.float32
    )


def thirds(value):
    parts = []
    for _ in range(3):
        part = value.astype(jnp.bfloat16)
        parts.append(part)
        value = value - part.astype(jnp.float32)
    return parts


def pack_own(cand_ref, ids_ref, lanczos_ref, weight_ref, out_ref, tail_ref,
             raw, ids, factor, weights, sems):
    rows, width = raw.shape
    rank = factor.shape[1]
    copies = [
        pltpu.make_async_copy(source, target, sems.at[i])
        for i, (source, target) in enumerate(
            ((cand_ref, raw), (ids_ref, ids), (lanczos_ref, factor), (weight_ref, weights))
        )
    ]
    for copy in copies:
        copy.start()
    for copy in copies:
        copy.wait()
    out_ref[:width, :] = unit_rows(raw[...]).T
    within = (ids[...] - ids[0, 0]).astype(jnp.float32)
    out_ref[width:, :] = jnp.broadcast_to(within, (TAIL, rows)).astype(jnp.bfloat16)
    tail_ref[:rank, :] = factor[...].T
    tail_ref[rank:, :] = jnp.broadcast_to(
        weights[...].astype(jnp.float32).reshape(1, -1), (TAIL, factor.shape[0])
    ).astype(jnp.bfloat16)


def pack_here(cand_ref, ids_ref, *rest):
    out_ref = rest[-1]
    rows, width = cand_ref.shape
    out_ref[:width, :] = unit_rows(cand_ref[...]).T
    within = (ids_ref[...] - ids_ref[0, 0]).astype(jnp.float32)
    out_ref[width:, :] = jnp.broadcast_to(within, (TAIL, rows)).astype(jnp.bfloat16)


def unit_train(own_ref, sib_ref, own_out, sib_out):
    step = own_ref.shape[0] // 6
    for raw, out in ((own_ref, own_out), (sib_ref, sib_out)):
        for i in range(6):
            part = slice(i * step, (i + 1) * step)
            out[part, :] = unit_rows(raw[part, :])


def copy_after(value_ref, *rest):
    rest[-1][...] = value_ref[...]


def quartic(products, width):
    cosine = products * (1.0 / width)
    square = cosine * cosine
    return square * square


def member_of(ref, base, count):
    ids = ref[ref.shape[0] - TAIL :, :][:1].astype(jnp.int32) + base
    row = lax.broadcasted_iota(jnp.int32, (count, ids.shape[1]), 0)
    return (row == ids).astype(jnp.bfloat16)


def project(masks, chips, width, rank, first, cut, parts, *rest):
    refs, (*train_refs, ) = rest[:parts], rest[parts : parts + 4]
    rest = rest[parts + 4 :]
    chip = lax.axis_index("train") // 2
    one, two = (
        jnp.concatenate([ref[...] for ref in piece], axis=0)
        for piece in (refs[:cut], refs[cut:])
    )
    pair = jnp.concatenate([one[:width, :], two[:width, :]], axis=1)
    structs = chips * SPB
    member = jnp.concatenate(
        [
            member_of(ref, lax.bitwise_xor(chip, mask) * SPB, structs)
            for ref, mask in zip((one, two), masks)
        ],
        axis=1,
    )
    proj = None
    for ref, tail in (train_refs[:2], train_refs[2:]):
        kernel_rows = quartic(product(ref[...], pair), width).astype(jnp.bfloat16)
        term = product(tail[...], kernel_rows)
        proj = term if proj is None else proj + term
    sums = sum(product(member, part, ((1,), (1,))) for part in thirds(proj))
    size = jnp.sum(member.astype(jnp.float32), axis=1, keepdims=True)
    sums = sums * (1.0 / jnp.maximum(size, 1.0))
    lane = lax.broadcasted_iota(jnp.int32, (SPB, TAIL), 1)
    means = jnp.zeros((SPB, TAIL), jnp.float32)
    for c in range(chips):
        means = jnp.where(lane == c, sums[c * SPB : (c + 1) * SPB, rank:], means)
    means = jnp.concatenate([means, jnp.zeros((SPB, rank - TAIL), jnp.float32)], axis=1)
    total = jnp.concatenate([sums[:, :rank], means], axis=0)
    if first:
        rest[0][...] = total
    else:
        rest[1][...] = rest[0][...] + total


def prior_part(masks, chips, width, first, cuts, own_ref, sib_ref, *rest):
    refs = []
    for cut in cuts:
        refs.append(jnp.concatenate([ref[...] for ref in rest[:cut]], axis=0))
        rest = rest[cut:]
    me = lax.axis_index("train")
    chip, core = me // 2, me % 2
    mine = jnp.concatenate([own_ref[:width, :], sib_ref[:width, :]], axis=1)
    none = jnp.zeros((SPB, own_ref.shape[1]), jnp.bfloat16)
    left = jnp.concatenate(
        [
            jnp.concatenate([member_of(own_ref, 0, SPB), none], axis=1),
            jnp.concatenate([none, member_of(sib_ref, 0, SPB)], axis=1),
        ],
        axis=0,
    )
    left_size = jnp.sum(left.astype(jnp.float32), axis=1, keepdims=True)
    total = None
    for i in range(0, len(masks), 2):
        two = refs[i : i + 2]
        pair = jnp.concatenate([ref[:width, :] for ref in two], axis=1)
        wide = jnp.concatenate(
            [
                member_of(ref, (lax.bitwise_xor(chip, mask) * 2 + core) * SPB, 2 * chips * SPB)
                for ref, mask in zip(two, masks[i : i + 2])
            ],
            axis=1,
        )
        wide_size = jnp.maximum(
            jnp.sum(wide.astype(jnp.float32), axis=1, keepdims=True), 1.0
        )
        pairs = quartic(product(mine, pair, ((0,), (0,))), width)
        half = sum(product(left, part) for part in thirds(pairs)) / left_size
        weight = thirds(wide.astype(jnp.float32) / wide_size)
        term = sum(
            product(a, b, ((1,), (1,)))
            for i, a in enumerate(thirds(half))
            for b in weight[: 3 - i]
        )
        total = term if total is None else total + term
    if first:
        rest[0][...] = total
    else:
        rest[1][...] = rest[0][...] + total


def last_sum(q_ref, more_ref, prior_ref, out_ref):
    rows = q_ref.shape[0]
    out_ref[:rows, :] = q_ref[...] + more_ref[...]
    for i in range(prior_ref.shape[1] // LANES):
        out_ref[rows + i * SPB : rows + (i + 1) * SPB, :] = prior_ref[
            SPB:, i * LANES : (i + 1) * LANES
        ]


def finish(q_ref, other_ref, prior_ref, mean_ref, cov_ref, all_ref):
    wide = prior_ref.shape[1]
    structs = wide // 2
    me = lax.axis_index("train")
    chip, core = me // 2, me % 2
    for p in range(structs // SPB):
        rows = slice(p * SPB, (p + 1) * SPB)
        here = pl.multiple_of((2 * p + core) * SPB, SPB)
        there = pl.multiple_of((2 * p + 1 - core) * SPB, SPB)
        all_ref[pl.ds(here, SPB), :] = q_ref[rows, :]
        all_ref[pl.ds(there, SPB), :] = other_ref[rows, :]
    own = thirds(q_ref[pl.ds(pl.multiple_of(chip * SPB, SPB), SPB), :])
    every = thirds(all_ref[...])
    square = sum(
        product(a, b, ((1,), (1,))) for i, a in enumerate(own) for b in every[: 3 - i]
    )
    start = structs + SPB
    theirs = [
        other_ref[start + i * SPB : start + (i + 1) * SPB, :] for i in range(wide // LANES)
    ]
    cov_ref[...] = prior_ref[:SPB, :] + jnp.concatenate(theirs, axis=1) - square
    lane = lax.broadcasted_iota(jnp.int32, (SPB, LANES), 1)
    row = lax.broadcasted_iota(jnp.int32, (SPB, LANES), 0)
    means = q_ref[structs:start, :]
    column = jnp.sum(jnp.where(lane == chip, means, 0.0), axis=1, keepdims=True)
    mean_ref[...] = jnp.sum(jnp.where(lane == row, column, 0.0), axis=0)[:SPB]


def call(kernel, shapes, count, flops=0, scratch=()):
    many = isinstance(shapes, (tuple, list))
    return pl.pallas_call(
        kernel,
        out_shape=shapes,
        in_specs=[VMEM] * count,
        out_specs=[VMEM] * len(shapes) if many else VMEM,
        scratch_shapes=scratch,
        cost_estimate=pl.CostEstimate(flops=flops, bytes_accessed=0, transcendentals=0),
        compiler_params=pltpu.CompilerParams(vmem_limit_bytes=24 * 2**20),
    )


def body(size, cand_desc, struct_id, train_desc, lanczos, mean_weight):
    rows, width = cand_desc.shape
    count, rank = lanczos.shape
    chips = size // 2
    structs = chips * SPB

    def swap(value, mask):
        return lax.ppermute(value, "train", [(i, i ^ mask) for i in range(size)])

    block_shape = jax.ShapeDtypeStruct((width + TAIL, rows), jnp.bfloat16)
    own, tail_own = pl.pallas_call(
        pack_own,
        out_shape=[
            block_shape,
            jax.ShapeDtypeStruct((rank + TAIL, count), jnp.bfloat16),
        ],
        in_specs=[HBM] * 4,
        out_specs=[VMEM] * 2,
        scratch_shapes=[
            pltpu.VMEM((rows, width), jnp.bfloat16),
            pltpu.VMEM((1, rows), jnp.int32),
            pltpu.VMEM((count, rank), jnp.bfloat16),
            pltpu.VMEM((count,), jnp.bfloat16),
            pltpu.SemaphoreType.DMA((4,)),
        ],
        compiler_params=pltpu.CompilerParams(vmem_limit_bytes=58 * 2**20),
    )(cand_desc, struct_id.reshape(1, rows), lanczos, mean_weight)

    def pack_received(mask, *others):
        return pl.pallas_call(
            pack_here,
            out_shape=block_shape,
            in_specs=[VMEM, VMEM] + [pl.BlockSpec(memory_space=pl.ANY)] * len(others),
            out_specs=VMEM,
            compiler_params=pltpu.CompilerParams(vmem_limit_bytes=24 * 2**20),
        )(swap(cand_desc, mask), swap(struct_id.reshape(1, rows), mask), *others)

    def again(value, *others):
        return pl.pallas_call(
            copy_after,
            out_shape=block_shape,
            in_specs=[VMEM] + [pl.BlockSpec(memory_space=pl.ANY)] * len(others),
            out_specs=VMEM,
            compiler_params=pltpu.CompilerParams(vmem_limit_bytes=24 * 2**20),
        )(value, *others)

    q_shape = jax.ShapeDtypeStruct((structs + SPB, rank), jnp.float32)
    prior_shape = jax.ShapeDtypeStruct((2 * SPB, 2 * structs), jnp.float32)

    def add_projection(masks, state, one, two):
        state = () if state is None else (state,)
        pair = (*one, *two)
        kernel = functools.partial(
            project, masks, chips, width, rank, not state, len(one), len(pair)
        )
        return call(
            kernel,
            q_shape,
            4 + len(pair) + len(state),
            flops=2 * 2 * rows * 2 * count * (width + 2 * rank),
        )(*pair, train_own, tail_own, train_sib, tail_sib, *state)

    def add_prior(masks, state, *refs):
        state = () if state is None else (state,)
        cuts = tuple(len(ref) for ref in refs)
        refs = [part for ref in refs for part in ref]
        kernel = functools.partial(prior_part, masks, chips, width, not state, cuts)
        return call(
            kernel,
            prior_shape,
            2 + len(refs) + len(state),
            flops=2 * 2 * rows * len(refs) * rows * (width + 2 * rank),
        )(own, sib, *refs, *state)

    blocks = {0: own}
    if size == 16:
        for mask in (2, 1):
            blocks[mask] = swap(own, 2 * mask)
    else:
        for mask in range(1, chips):
            blocks[mask] = swap(own, 2 * mask)
    train_shape = jax.ShapeDtypeStruct(train_desc.shape, jnp.bfloat16)
    train_own, train_sib = call(unit_train, (train_shape, train_shape), 2)(
        train_desc, swap(train_desc, 1)
    )
    tail_sib = swap(tail_own, 1)
    if size == 16:
        far = pack_received(8, train_own)
        blocks[4] = far
        blocks[6] = swap(far, 4)
        blocks[5] = swap(again(far, blocks[2]), 2)
        blocks[3] = swap(again(blocks[1], far), 4)
        blocks[7] = swap(blocks[6], 2)
        groups = ((0, 1), (2, 4), (5, 6), (3, 7))
    else:
        groups = [(m, m + 1) for m in range(0, chips, 2)]
    blocks = {m: b if isinstance(b, (tuple, list)) else (b,) for m, b in blocks.items()}
    q = None
    for one, two in groups:
        q = add_projection((one, two), q, blocks[one], blocks[two])
    sib = swap(own, 1)
    prior = add_prior(tuple(range(chips)), None, *[blocks[m] for m in range(chips)])

    mask = 2
    while mask < size // 2:
        q = q + swap(q, mask)
        mask *= 2
    tail = structs + SPB + 2 * structs // LANES * SPB
    q = call(last_sum, jax.ShapeDtypeStruct((tail, rank), jnp.float32), 3)(
        q, swap(q, mask), prior
    )
    mean, covariance = call(
        finish,
        (
            jax.ShapeDtypeStruct((SPB,), jnp.float32),
            jax.ShapeDtypeStruct((SPB, 2 * structs), jnp.float32),
        ),
        3,
        scratch=[pltpu.VMEM((2 * structs, rank), jnp.float32)],
    )(q, swap(q, 1), prior)
    return mean, covariance[None]


def solution(mesh):
    placed = (
        P(("pool", "cand", "train"), None),
        P(("pool", "cand", "train")),
        P(("pool", "train"), None),
        P(("pool", "train"), None),
        P(("pool", "train")),
    )
    return jax.shard_map(
        functools.partial(body, mesh.shape["train"]),
        mesh=mesh,
        in_specs=placed,
        out_specs=(P(("pool", "cand", "train")), P(("pool", "cand"), "train", None)),
        check_vma=False,
    )
```

```python
import functools

import jax
import jax.numpy as jnp
from jax import lax
from jax.experimental import pallas as pl
from jax.experimental.pallas import tpu as pltpu
from jax.sharding import PartitionSpec as P

SPB = 8
EPSILON = 1e-06
LANES = 128
TAIL = 16
VMEM = pl.BlockSpec(memory_space=pltpu.VMEM)
HBM = pl.BlockSpec(memory_space=pltpu.HBM)


def unit_rows(values):
    wide = values.astype(jnp.float32)
    scale = lax.rsqrt(jnp.mean(wide * wide, axis=1, keepdims=True) + EPSILON)
    return (wide * scale).astype(jnp.bfloat16)


def product(left, right, dims=((1,), (0,))):
    return lax.dot_general(
        left, right, (dims, ((), ())), preferred_element_type=jnp.float32
    )


def thirds(value):
    parts = []
    for _ in range(3):
        part = value.astype(jnp.bfloat16)
        parts.append(part)
        value = value - part.astype(jnp.float32)
    return parts


def pack_own(cand_ref, ids_ref, lanczos_ref, weight_ref, out_ref, tail_ref,
             raw, ids, factor, weights, sems):
    rows, width = raw.shape
    rank = factor.shape[1]
    copies = [
        pltpu.make_async_copy(source, target, sems.at[i])
        for i, (source, target) in enumerate(
            ((cand_ref, raw), (ids_ref, ids), (lanczos_ref, factor), (weight_ref, weights))
        )
    ]
    for copy in copies:
        copy.start()
    for copy in copies:
        copy.wait()
    out_ref[:width, :] = unit_rows(raw[...]).T
    within = (ids[...] - ids[0, 0]).astype(jnp.float32)
    out_ref[width:, :] = jnp.broadcast_to(within, (TAIL, rows)).astype(jnp.bfloat16)
    tail_ref[:rank, :] = factor[...].T
    tail_ref[rank:, :] = jnp.broadcast_to(
        weights[...].astype(jnp.float32).reshape(1, -1), (TAIL, factor.shape[0])
    ).astype(jnp.bfloat16)


def pack_here(cand_ref, ids_ref, *rest):
    out_ref = rest[-1]
    rows, width = cand_ref.shape
    out_ref[:width, :] = unit_rows(cand_ref[...]).T
    within = (ids_ref[...] - ids_ref[0, 0]).astype(jnp.float32)
    out_ref[width:, :] = jnp.broadcast_to(within, (TAIL, rows)).astype(jnp.bfloat16)


def unit_train(own_ref, sib_ref, own_out, sib_out):
    step = own_ref.shape[0] // 6
    for raw, out in ((own_ref, own_out), (sib_ref, sib_out)):
        for i in range(6):
            part = slice(i * step, (i + 1) * step)
            out[part, :] = unit_rows(raw[part, :])


def copy_after(value_ref, _, *out_refs):
    start = 0
    for ref in out_refs:
        ref[...] = value_ref[start : start + ref.shape[0], :]
        start += ref.shape[0]


def quartic(products, width):
    cosine = products * (1.0 / width)
    square = cosine * cosine
    return square * square


def member_of(ref, base, count):
    ids = ref[ref.shape[0] - TAIL :, :][:1].astype(jnp.int32) + base
    row = lax.broadcasted_iota(jnp.int32, (count, ids.shape[1]), 0)
    return (row == ids).astype(jnp.bfloat16)


def project(masks, chips, width, rank, first, cut, parts, *rest):
    refs, (*train_refs, ) = rest[:parts], rest[parts : parts + 4]
    rest = rest[parts + 4 :]
    chip = lax.axis_index("train") // 2
    one, two = (
        jnp.concatenate([ref[...] for ref in piece], axis=0)
        for piece in (refs[:cut], refs[cut:])
    )
    pair = jnp.concatenate([one[:width, :], two[:width, :]], axis=1)
    structs = chips * SPB
    member = jnp.concatenate(
        [
            member_of(ref, lax.bitwise_xor(chip, mask) * SPB, structs)
            for ref, mask in zip((one, two), masks)
        ],
        axis=1,
    )
    proj = None
    for ref, tail in (train_refs[:2], train_refs[2:]):
        kernel_rows = quartic(product(ref[...], pair), width).astype(jnp.bfloat16)
        term = product(tail[...], kernel_rows)
        proj = term if proj is None else proj + term
    sums = sum(product(member, part, ((1,), (1,))) for part in thirds(proj))
    size = jnp.sum(member.astype(jnp.float32), axis=1, keepdims=True)
    sums = sums * (1.0 / jnp.maximum(size, 1.0))
    lane = lax.broadcasted_iota(jnp.int32, (SPB, TAIL), 1)
    means = jnp.zeros((SPB, TAIL), jnp.float32)
    for c in range(chips):
        means = jnp.where(lane == c, sums[c * SPB : (c + 1) * SPB, rank:], means)
    means = jnp.concatenate([means, jnp.zeros((SPB, rank - TAIL), jnp.float32)], axis=1)
    total = jnp.concatenate([sums[:, :rank], means], axis=0)
    if first:
        rest[0][...] = total
    else:
        rest[1][...] = rest[0][...] + total


def prior_part(masks, chips, width, first, cuts, own_ref, sib_ref, *rest):
    refs = []
    for cut in cuts:
        refs.append(jnp.concatenate([ref[...] for ref in rest[:cut]], axis=0))
        rest = rest[cut:]
    me = lax.axis_index("train")
    chip, core = me // 2, me % 2
    mine = jnp.concatenate([own_ref[:width, :], sib_ref[:width, :]], axis=1)
    none = jnp.zeros((SPB, own_ref.shape[1]), jnp.bfloat16)
    left = jnp.concatenate(
        [
            jnp.concatenate([member_of(own_ref, 0, SPB), none], axis=1),
            jnp.concatenate([none, member_of(sib_ref, 0, SPB)], axis=1),
        ],
        axis=0,
    )
    left_size = jnp.sum(left.astype(jnp.float32), axis=1, keepdims=True)
    total = None
    for i in range(0, len(masks), 2):
        two = refs[i : i + 2]
        pair = jnp.concatenate([ref[:width, :] for ref in two], axis=1)
        wide = jnp.concatenate(
            [
                member_of(ref, (lax.bitwise_xor(chip, mask) * 2 + core) * SPB, 2 * chips * SPB)
                for ref, mask in zip(two, masks[i : i + 2])
            ],
            axis=1,
        )
        wide_size = jnp.maximum(
            jnp.sum(wide.astype(jnp.float32), axis=1, keepdims=True), 1.0
        )
        pairs = quartic(product(mine, pair, ((0,), (0,))), width)
        half = sum(product(left, part) for part in thirds(pairs)) / left_size
        weight = thirds(wide.astype(jnp.float32) / wide_size)
        term = sum(
            product(a, b, ((1,), (1,)))
            for i, a in enumerate(thirds(half))
            for b in weight[: 3 - i]
        )
        total = term if total is None else total + term
    if first:
        rest[0][...] = total
    else:
        rest[1][...] = rest[0][...] + total


def last_sum(q_ref, more_ref, prior_ref, out_ref):
    rows = q_ref.shape[0]
    out_ref[:rows, :] = q_ref[...] + more_ref[...]
    for i in range(prior_ref.shape[1] // LANES):
        out_ref[rows + i * SPB : rows + (i + 1) * SPB, :] = prior_ref[
            SPB:, i * LANES : (i + 1) * LANES
        ]


def finish(q_ref, other_ref, prior_ref, mean_ref, cov_ref, all_ref):
    wide = prior_ref.shape[1]
    structs = wide // 2
    me = lax.axis_index("train")
    chip, core = me // 2, me % 2
    for p in range(structs // SPB):
        rows = slice(p * SPB, (p + 1) * SPB)
        here = pl.multiple_of((2 * p + core) * SPB, SPB)
        there = pl.multiple_of((2 * p + 1 - core) * SPB, SPB)
        all_ref[pl.ds(here, SPB), :] = q_ref[rows, :]
        all_ref[pl.ds(there, SPB), :] = other_ref[rows, :]
    own = thirds(q_ref[pl.ds(pl.multiple_of(chip * SPB, SPB), SPB), :])
    every = thirds(all_ref[...])
    square = sum(
        product(a, b, ((1,), (1,))) for i, a in enumerate(own) for b in every[: 3 - i]
    )
    start = structs + SPB
    theirs = [
        other_ref[start + i * SPB : start + (i + 1) * SPB, :] for i in range(wide // LANES)
    ]
    cov_ref[...] = prior_ref[:SPB, :] + jnp.concatenate(theirs, axis=1) - square
    lane = lax.broadcasted_iota(jnp.int32, (SPB, LANES), 1)
    row = lax.broadcasted_iota(jnp.int32, (SPB, LANES), 0)
    means = q_ref[structs:start, :]
    column = jnp.sum(jnp.where(lane == chip, means, 0.0), axis=1, keepdims=True)
    mean_ref[...] = jnp.sum(jnp.where(lane == row, column, 0.0), axis=0)[:SPB]


def call(kernel, shapes, count, flops=0, scratch=()):
    many = isinstance(shapes, (tuple, list))
    return pl.pallas_call(
        kernel,
        out_shape=shapes,
        in_specs=[VMEM] * count,
        out_specs=[VMEM] * len(shapes) if many else VMEM,
        scratch_shapes=scratch,
        cost_estimate=pl.CostEstimate(flops=flops, bytes_accessed=0, transcendentals=0),
        compiler_params=pltpu.CompilerParams(vmem_limit_bytes=24 * 2**20),
    )


def body(size, cand_desc, struct_id, train_desc, lanczos, mean_weight):
    rows, width = cand_desc.shape
    count, rank = lanczos.shape
    chips = size // 2
    structs = chips * SPB

    def swap(value, mask):
        return lax.ppermute(value, "train", [(i, i ^ mask) for i in range(size)])

    block_shape = jax.ShapeDtypeStruct((width + TAIL, rows), jnp.bfloat16)
    own, tail_own = pl.pallas_call(
        pack_own,
        out_shape=[
            block_shape,
            jax.ShapeDtypeStruct((rank + TAIL, count), jnp.bfloat16),
        ],
        in_specs=[HBM] * 4,
        out_specs=[VMEM] * 2,
        scratch_shapes=[
            pltpu.VMEM((rows, width), jnp.bfloat16),
            pltpu.VMEM((1, rows), jnp.int32),
            pltpu.VMEM((count, rank), jnp.bfloat16),
            pltpu.VMEM((count,), jnp.bfloat16),
            pltpu.SemaphoreType.DMA((4,)),
        ],
        compiler_params=pltpu.CompilerParams(vmem_limit_bytes=58 * 2**20),
    )(cand_desc, struct_id.reshape(1, rows), lanczos, mean_weight)

    def again(value, other, pieces):
        shapes = [
            jax.ShapeDtypeStruct((piece, value.shape[1]), value.dtype) for piece in pieces
        ]
        return pl.pallas_call(
            copy_after,
            out_shape=shapes,
            in_specs=[VMEM, pl.BlockSpec(memory_space=pl.ANY)],
            out_specs=[VMEM] * len(shapes),
            compiler_params=pltpu.CompilerParams(vmem_limit_bytes=24 * 2**20),
        )(value, other)

    def again_last(value, *others):
        return pl.pallas_call(
            lambda *refs: copy_after(refs[-2], None, refs[-1]),
            out_shape=block_shape,
            in_specs=[pl.BlockSpec(memory_space=pl.ANY)] * len(others) + [VMEM],
            out_specs=VMEM,
            compiler_params=pltpu.CompilerParams(vmem_limit_bytes=24 * 2**20),
        )(*others, value)

    def pack_received(mask, *others):
        return pl.pallas_call(
            pack_here,
            out_shape=block_shape,
            in_specs=[VMEM, VMEM] + [pl.BlockSpec(memory_space=pl.ANY)] * len(others),
            out_specs=VMEM,
            compiler_params=pltpu.CompilerParams(vmem_limit_bytes=24 * 2**20),
        )(swap(cand_desc, mask), swap(struct_id.reshape(1, rows), mask), *others)

    def again_pieces(value, pieces, *others):
        shapes = [
            jax.ShapeDtypeStruct((piece, value.shape[1]), value.dtype) for piece in pieces
        ]
        def kernel(*refs):
            refs[1 + len(others)][...] = refs[0][...]
            copy_after(refs[0], None, *refs[2 + len(others) :])
        return pl.pallas_call(
            kernel,
            out_shape=[block_shape, *shapes],
            in_specs=[VMEM] + [pl.BlockSpec(memory_space=pl.ANY)] * len(others),
            out_specs=[VMEM] * (1 + len(shapes)),
            compiler_params=pltpu.CompilerParams(vmem_limit_bytes=24 * 2**20),
        )(value, *others)

    def again_first(value, *others):
        return pl.pallas_call(
            lambda *refs: copy_after(refs[0], None, refs[-1]),
            out_shape=block_shape,
            in_specs=[VMEM] + [pl.BlockSpec(memory_space=pl.ANY)] * len(others),
            out_specs=VMEM,
            compiler_params=pltpu.CompilerParams(vmem_limit_bytes=24 * 2**20),
        )(value, *others)

    q_shape = jax.ShapeDtypeStruct((structs + SPB, rank), jnp.float32)
    prior_shape = jax.ShapeDtypeStruct((2 * SPB, 2 * structs), jnp.float32)

    def add_projection(masks, state, one, two):
        state = () if state is None else (state,)
        pair = (*one, *two)
        kernel = functools.partial(
            project, masks, chips, width, rank, not state, len(one), len(pair)
        )
        return call(
            kernel,
            q_shape,
            4 + len(pair) + len(state),
            flops=2 * 2 * rows * 2 * count * (width + 2 * rank),
        )(*pair, train_own, tail_own, train_sib, tail_sib, *state)

    def add_prior(masks, state, *refs):
        state = () if state is None else (state,)
        cuts = tuple(len(ref) for ref in refs)
        refs = [part for ref in refs for part in ref]
        kernel = functools.partial(prior_part, masks, chips, width, not state, cuts)
        return call(
            kernel,
            prior_shape,
            2 + len(refs) + len(state),
            flops=2 * 2 * rows * len(refs) * rows * (width + 2 * rank),
        )(own, sib, *refs, *state)

    blocks = {0: own}
    if size == 16:
        for mask in (2, 1):
            blocks[mask] = swap(own, 2 * mask)
    else:
        for mask in range(1, chips):
            blocks[mask] = swap(own, 2 * mask)
    train_shape = jax.ShapeDtypeStruct(train_desc.shape, jnp.bfloat16)
    train_own, train_sib = call(unit_train, (train_shape, train_shape), 2)(
        train_desc, swap(train_desc, 1)
    )
    tail_sib = swap(tail_own, 1)
    if size == 16:
        far = pack_received(8, train_own)
        blocks[4] = far
        blocks[6] = swap(far, 4)
        blocks[5] = swap(again_first(far, blocks[2]), 2)
        groups = ((0, 1), (2, 5), (4, 6), (3, 7))
    else:
        groups = [(m, m + 1) for m in range(0, chips, 2)]
    blocks = {m: b if isinstance(b, (tuple, list)) else (b,) for m, b in blocks.items()}
    q = None
    for one, two in groups:
        q = add_projection((one, two), q, blocks[one], blocks[two])
        if size == 16 and (one, two) == groups[0]:
            blocks[3] = (swap(again_first(blocks[1][0], q), 4),)
        if size == 16 and (one, two) == groups[0]:
            blocks[7] = (swap(again_first(blocks[6][0], q), 2),)
    sib = swap(own, 1)
    prior = add_prior(tuple(range(chips)), None, *[blocks[m] for m in range(chips)])

    mask = 2
    while mask < size // 2:
        q = q + swap(q, mask)
        mask *= 2
    tail = structs + SPB + 2 * structs // LANES * SPB
    q = call(last_sum, jax.ShapeDtypeStruct((tail, rank), jnp.float32), 3)(
        q, swap(q, mask), prior
    )
    mean, covariance = call(
        finish,
        (
            jax.ShapeDtypeStruct((SPB,), jnp.float32),
            jax.ShapeDtypeStruct((SPB, 2 * structs), jnp.float32),
        ),
        3,
        scratch=[pltpu.VMEM((2 * structs, rank), jnp.float32)],
    )(q, swap(q, 1), prior)
    return mean, covariance[None]


def solution(mesh):
    placed = (
        P(("pool", "cand", "train"), None),
        P(("pool", "cand", "train")),
        P(("pool", "train"), None),
        P(("pool", "train"), None),
        P(("pool", "train")),
    )
    return jax.shard_map(
        functools.partial(body, mesh.shape["train"]),
        mesh=mesh,
        in_specs=placed,
        out_specs=(P(("pool", "cand", "train")), P(("pool", "cand"), "train", None)),
        check_vma=False,
    )
```
